512 devices in a mesh: outer: 64 (over z, y_hi, core), inner: 8 (over y_lo, x).
Axes of the slice: x: 4, y: 4 (y_hi: 2, y_lo: 2; y = y_hi * 2 + y_lo), z: 16, core: 2. Of those that a mesh axis runs over, the one named last changes fastest.
Arguments:
- queries: bfloat16 [131072, 1024], P(('outer', 'inner')), may hold values from -6 to 6
- keys: bfloat16 [131072, 1024], P(('outer', 'inner')), may hold values from -6 to 6
- values: bfloat16 [131072, 1024], P(('outer', 'inner')), may hold values from -6 to 6
Outputs:
- attended: bfloat16 [131072, 1024], P(('outer', 'inner'))
The draws below stay inside these ranges and needn't reach their ends.
All inputs are finite; a program needn't handle non-finite values.
Results may differ from the reference program's by a relative error of at most 0.0029.
Values may be sent and summed in bfloat16 or wider, within the bound.
No kernel may reach another device: no remote copies, remote signals or barrier semaphores. Data moves between devices by JAX's collectives and lax.ppermute only.
A program may use at most 64 MiB of HBM per device.

```python
import jax
import jax.numpy as jnp
from jax import lax

LOCAL_HEADS = 8
HEAD_DIM = 128
SECOND_DILATION = 8
THIRD_DILATION = 64
FIRST_SEGMENT = 2048
SECOND_SEGMENT = 16384
TOKENS = 131072


def draw_queries(key, part):
    key = jax.random.fold_in(key, 11)
    result = jnp.clip(1.7 * jax.random.normal(key, (TOKENS, LOCAL_HEADS * HEAD_DIM), jnp.float32), -6.0, 6.0)
    return result.astype(jnp.bfloat16)


def draw_keys(key, part):
    key = jax.random.fold_in(key, 23)
    result = jnp.clip(1.7 * jax.random.normal(key, (TOKENS, LOCAL_HEADS * HEAD_DIM), jnp.float32), -6.0, 6.0)
    return result.astype(jnp.bfloat16)


def block_levels(stream_key, shape, cuts, least, high):
    def one(dim, parts):
        steps = jax.random.uniform(jax.random.fold_in(jax.random.fold_in(stream_key, 6), dim), (parts,), jnp.float32, least / len(cuts), high / len(cuts))
        return jnp.repeat(jnp.exp(steps), shape[dim] // parts).reshape((-1,) + (1,) * (len(shape) - dim - 1))

    level = one(*cuts[0])
    for cut in cuts[1:]:
        level = level * one(*cut)
    return level


def noise(key, dims, scale, reach, shards=(), kind=jnp.bfloat16):
    array = scale * jax.random.normal(key, dims, jnp.float32)
    if shards:
        array = array * block_levels(key, dims, shards, -0.22, 0.18)
    return jnp.clip(array, -reach, reach).astype(kind)


def setup_inputs(seed: int = 0) -> dict:
    key_list = jax.random.split(jax.random.key(seed), 4)
    return {
        "queries": draw_queries(jax.random.fold_in(key_list[3], 71), 0),
        "keys": draw_keys(jax.random.fold_in(key_list[3], 71), 0),
        "values": noise(key_list[2], (TOKENS, LOCAL_HEADS * HEAD_DIM), 1.0, 6.0, ((0, 512),)),
    }


def attend_head(q_head, k_head, v_head):
    scaling = q_head.shape[1] ** -0.5
    scores = lax.dot_general(q_head, k_head, (((1,), (1,)), ((), ())), preferred_element_type=jnp.float32) * scaling
    peak_now = jnp.max(scores, axis=1)
    weights = jnp.exp(scores - peak_now[:, None])
    total_list = jnp.sum(weights, axis=1)
    summed_output = jnp.dot(weights.astype(jnp.bfloat16), v_head, preferred_element_type=jnp.float32)
    return peak_now, total_list, summed_output


def level_stats(queries, keys, values, device_heads):
    head_width = queries.shape[1] // device_heads

    def one_head(head_no):
        start = head_no * head_width
        return attend_head(lax.dynamic_slice_in_dim(queries, start, head_width, 1),
                           lax.dynamic_slice_in_dim(keys, start, head_width, 1),
                           lax.dynamic_slice_in_dim(values, start, head_width, 1))

    peak_now, total_list, summed_output = lax.map(one_head, jnp.arange(device_heads, dtype=jnp.int32))
    return peak_now.T, total_list.T, jnp.swapaxes(summed_output, 0, 1)


def select_rows(rows, rate, leading_head, device_heads):
    head_width = rows.shape[1] // device_heads
    blocks = rows.shape[0] // rate
    layout = rows.reshape(blocks, rate, device_heads, head_width)
    window = lax.dynamic_slice_in_dim(layout, leading_head, device_heads, 1)
    picked = jnp.diagonal(window, axis1=1, axis2=2)
    return jnp.swapaxes(picked, 1, 2).reshape(blocks, device_heads * head_width)


def merge_level(current_maximum, total_list, summed_output, top_add, total_add, sum_add, rate, leading_head):
    device_heads = current_maximum.shape[1]
    blocks = current_maximum.shape[0] // rate
    head_width = summed_output.shape[2]
    chosen = jnp.arange(rate, dtype=jnp.int32)[:, None] == (leading_head + jnp.arange(device_heads, dtype=jnp.int32))[None, :]
    base_top = current_maximum.reshape(blocks, rate, device_heads)
    extra_top = top_add[:, None, :]
    peak_now = jnp.where(chosen, jnp.maximum(base_top, extra_top), base_top)
    near_w = jnp.exp(base_top - peak_now)
    far_w = jnp.where(chosen, jnp.exp(extra_top - peak_now), 0.0)
    new_total = near_w * total_list.reshape(blocks, rate, device_heads) + far_w * total_add[:, None, :]
    new_sum = near_w[..., None] * summed_output.reshape(blocks, rate, device_heads, head_width) + far_w[..., None] * sum_add[:, None, :, :]
    return peak_now.reshape(-1, device_heads), new_total.reshape(-1, device_heads), new_sum.reshape(-1, device_heads, head_width)


def finish_rows(total_list, summed_output):
    return (summed_output / total_list[..., None]).reshape(summed_output.shape[0], -1).astype(jnp.bfloat16)


def reference(queries, keys, values):
    middle_rows = [select_rows(source_rows, SECOND_DILATION, 0, LOCAL_HEADS) for source_rows in (queries, keys, values)]
    distant_rows = [select_rows(source_rows, THIRD_DILATION, 0, LOCAL_HEADS) for source_rows in (queries, keys, values)]
    distant_maximum, distant_total, distant_sum = level_stats(distant_rows[0], distant_rows[1], distant_rows[2], LOCAL_HEADS)
    group_row_list = SECOND_SEGMENT // SECOND_DILATION

    def one_group(group_no):
        start = group_no * group_row_list
        parts_now = [lax.dynamic_slice_in_dim(source_rows, start, group_row_list, 0) for source_rows in middle_rows]
        return level_stats(parts_now[0], parts_now[1], parts_now[2], LOCAL_HEADS)

    middle_maximum, middle_total, middle_sum = lax.map(one_group, jnp.arange(TOKENS // SECOND_SEGMENT, dtype=jnp.int32))
    middle_maximum = middle_maximum.reshape(-1, LOCAL_HEADS)
    middle_total = middle_total.reshape(-1, LOCAL_HEADS)
    middle_sum = middle_sum.reshape(-1, LOCAL_HEADS, HEAD_DIM)
    segment_middle = FIRST_SEGMENT // SECOND_DILATION
    segment_distant = FIRST_SEGMENT // THIRD_DILATION

    def one_segment(seg_index):
        start = seg_index * FIRST_SEGMENT
        segment_query = lax.dynamic_slice_in_dim(queries, start, FIRST_SEGMENT, 0)
        segment_key = lax.dynamic_slice_in_dim(keys, start, FIRST_SEGMENT, 0)
        segment_value = lax.dynamic_slice_in_dim(values, start, FIRST_SEGMENT, 0)
        current_maximum, total_list, summed_output = level_stats(segment_query, segment_key, segment_value, LOCAL_HEADS)
        middle_floor = seg_index * segment_middle
        current_maximum, total_list, summed_output = merge_level(current_maximum, total_list, summed_output,
                                              lax.dynamic_slice_in_dim(middle_maximum, middle_floor, segment_middle, 0),
                                              lax.dynamic_slice_in_dim(middle_total, middle_floor, segment_middle, 0),
                                              lax.dynamic_slice_in_dim(middle_sum, middle_floor, segment_middle, 0), SECOND_DILATION, 0)
        distant_floor = seg_index * segment_distant
        current_maximum, total_list, summed_output = merge_level(current_maximum, total_list, summed_output,
                                              lax.dynamic_slice_in_dim(distant_maximum, distant_floor, segment_distant, 0),
                                              lax.dynamic_slice_in_dim(distant_total, distant_floor, segment_distant, 0),
                                              lax.dynamic_slice_in_dim(distant_sum, distant_floor, segment_distant, 0), THIRD_DILATION, 0)
        return finish_rows(total_list, summed_output)

    blocks = lax.map(one_segment, jnp.arange(TOKENS // FIRST_SEGMENT, dtype=jnp.int32))
    return blocks.reshape(TOKENS, LOCAL_HEADS * HEAD_DIM)
```

```python
import functools
import math

import jax
import jax.numpy as jnp
from jax import lax
from jax.experimental import pallas as pl
from jax.experimental.pallas import tpu as pltpu
from jax.sharding import PartitionSpec as P

D = 128
HEADS = 8
ROWS = 256
SLOTS = 32
FAR = 4
NEAR = 8
GROUPS = 8
SCALE = D**-0.5 * math.log2(math.e)
LIMIT = 48 << 20

NT = (((1,), (1,)), ((), ()))
F32 = jnp.float32
BF16 = jnp.bfloat16


def place(t, head):
    u = t >> 3
    return (((t - head) & 7) << 5) + ((u & 7) << 2) + (u >> 3)


def to_order(head):
    p = lax.broadcasted_iota(jnp.int32, (ROWS, ROWS), 0)
    t = lax.broadcasted_iota(jnp.int32, (1, ROWS), 1)
    return jnp.where(p == place(t, head), 1.0, 0.0).astype(BF16)


def from_order(head):
    p = lax.broadcasted_iota(jnp.int32, (ROWS, ROWS), 1)
    t = lax.broadcasted_iota(jnp.int32, (ROWS, 1), 0)
    return jnp.where(p == place(t, head), 1.0, 0.0).astype(BF16)


def dot(a, b):
    return jnp.dot(a, b, preferred_element_type=F32)


def split_kv(q_ref, k_ref, v_ref, kv_ref, q3_ref):
    third = jnp.zeros((HEADS * FAR, D), F32)
    r = lax.broadcasted_iota(jnp.int32, (HEADS * FAR, ROWS), 0)
    t = lax.broadcasted_iota(jnp.int32, (HEADS * FAR, ROWS), 1)
    for h in range(HEADS):
        order = to_order(h)
        cols = slice(h * D, (h + 1) * D)
        both = jnp.concatenate([k_ref[:, cols], v_ref[:, cols]], axis=1)
        out = dot(order, both).astype(BF16)
        kv_ref[h, 0] = out[:, :D]
        kv_ref[h, 1] = out[:, D:]
        pick = jnp.where((t == 64 * (r & 3) + h) & ((r >> 2) == h), 1.0, 0.0).astype(BF16)
        third = third + dot(pick, q_ref[:, cols])
    q3_ref[...] = third.astype(BF16)


def split_q(q_ref, q3_ref, out_ref):
    for h in range(HEADS):
        cols = slice(h * D, (h + 1) * D)
        out_ref[h, :ROWS] = dot(to_order(h), q_ref[:, cols]).astype(BF16)
    a = lax.broadcasted_iota(jnp.int32, (ROWS, ROWS), 0)
    b = lax.broadcasted_iota(jnp.int32, (ROWS, ROWS), 1)
    src = (((a >> 2) & 7) << 5) + ((a >> 5) << 2) + (a & 3)
    moved = dot(jnp.where(b == src, 1.0, 0.0).astype(BF16), q3_ref[...]).astype(BF16)
    for h in range(HEADS):
        out_ref[h, ROWS:] = moved[h * 32 : (h + 1) * 32]


def pick_chosen(kv_ref, kv2_ref, far_ref):
    kv2 = kv_ref[...]
    kv2_ref[...] = kv2
    a = lax.broadcasted_iota(jnp.int32, (HEADS * FAR, ROWS), 0)
    b = lax.broadcasted_iota(jnp.int32, (HEADS * FAR, ROWS), 1)
    pick = jnp.where(b == ((a >> 2) << 5) + (a & 3), 1.0, 0.0).astype(BF16)
    k3 = dot(pick, kv2[:, 0].reshape(ROWS, D)).astype(BF16)
    v3 = dot(pick, kv2[:, 1].reshape(ROWS, D)).astype(BF16)
    for g in range(GROUPS):
        far_ref[g, 0] = k3
        far_ref[g, 1] = v3


def two_parts(q):
    scaled = q.astype(F32) * SCALE
    high = scaled.astype(BF16)
    low = (scaled - high.astype(F32)).astype(BF16)
    return jnp.concatenate([high, low], axis=1)


def twice(k):
    return jnp.concatenate([k, k], axis=1)


def with_ones(v):
    return jnp.concatenate([v, jnp.ones_like(v)], axis=1)


def attend(q, keys, values):
    s = lax.dot_general(q, keys, NT, preferred_element_type=F32)
    top = jnp.max(s, axis=1, keepdims=True)
    w = jnp.exp2(s - top).astype(BF16)
    o = dot(w, values)
    return jnp.broadcast_to(top, (q.shape[0], D)), o[:, D:], o[:, :D]


def first_level(q_ref, kv_ref, o_ref, stat_ref, k_scr, v_scr):
    for s in range(HEADS):
        rows = slice(s * ROWS, (s + 1) * ROWS)
        k_scr[rows, :] = twice(kv_ref[s, 0])
        v_scr[rows, :] = with_ones(kv_ref[s, 1])

    def step(s, _):
        top, total, part = attend(two_parts(q_ref[s, :ROWS]), k_scr[...], v_scr[...])
        o_ref[s] = (part / total).astype(BF16)
        stat_ref[0, s] = top[:SLOTS]
        stat_ref[1, s] = total[:SLOTS]
        stat_ref[2, s] = part[:SLOTS]
        return 0

    lax.fori_loop(0, HEADS, step, 0)


def merge(top_a, total_a, part_a, top_b, total_b, part_b):
    peak = jnp.maximum(top_a, top_b)
    a, b = jnp.exp2(top_a - peak), jnp.exp2(top_b - peak)
    return peak, a * total_a + b * total_b, a * part_a + b * part_b


def later_levels(own_ref, q_ref, q3_ref, here_ref, there_ref, far_ref, stat_ref, o_in, o_ref, third_ref, k_scr, v_scr):
    n = NEAR // 2 * ROWS
    for s in range(NEAR // 2):
        for i, ref in enumerate((here_ref, there_ref)):
            at = i * n + s * ROWS
            k_scr[at : at + ROWS, :] = twice(ref[s, :, 0].reshape(ROWS, D))
            v_scr[at : at + ROWS, :] = with_ones(ref[s, :, 1].reshape(ROWS, D))
    q = two_parts(q_ref[...].reshape(ROWS, D))
    level2 = attend(q, k_scr[...], v_scr[...])
    first = [stat_ref[i].reshape(ROWS, D) for i in range(3)]
    top, total, part = merge(*first, *level2)
    o_ref[...] = (part / total).astype(BF16).reshape(HEADS, SLOTS, D)
    a = lax.broadcasted_iota(jnp.int32, (2 * ROWS, ROWS), 0)
    b = lax.broadcasted_iota(jnp.int32, (2 * ROWS, ROWS), 1)
    src = (((a >> 3) & 7) << 5) + ((a >> 6) << 2) + (a & 3)
    q3 = dot(jnp.where(b == src, 1.0, 0.0).astype(BF16), q3_ref[...].reshape(ROWS, D)).astype(BF16)
    k3, v3 = far_ref[:, 0].reshape(ROWS, D), far_ref[:, 1].reshape(ROWS, D)
    top3, total3, part3 = attend(two_parts(q3), twice(k3), with_ones(v3))
    row = lax.broadcasted_iota(jnp.int32, (HEADS * 8, D), 0) & 7

    def both(x):
        x = x.reshape(HEADS, SLOTS, D)[:, :8].reshape(HEADS * 8, D)
        turned = pltpu.roll(x, 4, 0)
        return jnp.where(row < 4, x, turned)

    mine = [both(x) for x in (top, total, part)]
    for j in range(NEAR):
        rows = slice(j * 64, (j + 1) * 64)
        third = [x[rows] for x in (top3, total3, part3)]
        merged = merge(*mine, *third)
        own = own_ref[0] == j
        t, l, o = [jnp.where(own, x, y) for x, y in zip(merged, third)]
        third_ref[j] = jnp.where(row < 4, o / l, t + jnp.log2(l)).reshape(HEADS, 8, D)


def finish(o_ref, third_ref, out_ref):
    parts = third_ref[...].reshape(NEAR, HEADS * 8, D)
    lse = [pltpu.roll(parts[j], HEADS * 8 - 4, 0) for j in range(NEAR)]
    peak = functools.reduce(jnp.maximum, lse)
    weights = [jnp.exp2(x - peak) for x in lse]
    total = sum(weights)
    merged = sum(w * parts[j] for j, w in enumerate(weights)) / total
    merged = merged.reshape(HEADS, 8, D)
    row = lax.broadcasted_iota(jnp.int32, (16, D), 0)
    for h in range(HEADS):
        head = o_ref[h]
        fixed = jnp.concatenate([merged[h], merged[h]], axis=0).astype(BF16)
        start = jnp.where(row < FAR, fixed, head[:16])
        head = jnp.concatenate([start, head[16:]], axis=0)
        out_ref[:, h * D : (h + 1) * D] = dot(from_order(h), head).astype(BF16)


def vmem(n):
    return [pl.BlockSpec(memory_space=pltpu.VMEM)] * n


def call(kernel, outs, ins, scratch=(), in_specs=None, out_specs=None, aliases=None, flops=0, grid=None):
    shapes = [jax.ShapeDtypeStruct(s, d) for s, d in outs]
    extra = {} if grid is None else {"grid": grid}
    got = pl.pallas_call(
        kernel,
        out_shape=shapes,
        in_specs=in_specs or vmem(len(ins)),
        out_specs=out_specs or vmem(len(outs)),
        scratch_shapes=list(scratch),
        input_output_aliases=aliases or {},
        compiler_params=pltpu.CompilerParams(vmem_limit_bytes=LIMIT),
        cost_estimate=pl.CostEstimate(flops=flops, bytes_accessed=1 << 20, transcendentals=0),
        **extra,
    )(*ins)
    return got if len(outs) > 1 else got[0]


def body(queries, keys, values):
    outer = lax.axis_size("outer")
    groups = outer // NEAR
    near = [[g * NEAR + j for j in range(NEAR)] for g in range(groups)]
    far = [[g * NEAR + j for g in range(groups)] for j in range(NEAR)]
    same_core = [[g * NEAR + 2 * m + c for m in range(NEAR // 2)] for g in range(groups) for c in range(2)]
    wide = [[g * NEAR * HEADS + i for i in range(NEAR * HEADS)] for g in range(groups)]
    own = (lax.axis_index("outer") % NEAR).astype(jnp.int32).reshape(1)

    kv, q3 = call(
        split_kv,
        [((HEADS, 2, ROWS, D), BF16), ((HEADS * FAR, D), BF16)],
        (queries, keys, values),
    )
    q3_near = lax.all_gather(q3, "outer", axis=0, tiled=True, axis_index_groups=near)
    kv = lax.all_to_all(kv, "inner", 0, 0, tiled=True)
    q = call(split_q, [((HEADS, ROWS + 32, D), BF16)], (queries, q3_near))
    q = lax.all_to_all(q, "inner", 0, 0, tiled=True)
    chosen, far_kv = call(
        pick_chosen,
        [((HEADS, 2, SLOTS, D), BF16), ((GROUPS, 2, 32, D), BF16)],
        (kv,),
        grid=(1,),
        in_specs=[pl.BlockSpec((HEADS, 2, SLOTS, D), lambda i: (0, 0, 0, 0))],
        out_specs=[
            pl.BlockSpec((HEADS, 2, SLOTS, D), lambda i: (0, 0, 0, 0)),
            pl.BlockSpec((GROUPS, 2, 32, D), lambda i: (0, 0, 0, 0)),
        ],
    )
    here = lax.all_gather(chosen[None], "outer", axis=0, tiled=True, axis_index_groups=same_core)
    there = lax.ppermute(here, "outer", [(i, i ^ 1) for i in range(outer)])
    far_kv = lax.all_to_all(far_kv, "outer", 0, 0, tiled=True, axis_index_groups=far)
    o, stat = call(
        first_level,
        [((HEADS, ROWS, D), BF16), ((3, HEADS, SLOTS, D), F32)],
        (q, kv),
        scratch=[pltpu.VMEM((HEADS * ROWS, 2 * D), BF16), pltpu.VMEM((HEADS * ROWS, 2 * D), BF16)],
        flops=1 << 33,
    )
    whole = lambda *shape: pl.BlockSpec(shape, lambda i: (0,) * len(shape))
    o, third = call(
        later_levels,
        [((HEADS, ROWS, D), BF16), ((NEAR, HEADS, 8, D), F32)],
        (own, q, q, here, there, far_kv, stat, o),
        scratch=[pltpu.VMEM((HEADS * ROWS, 2 * D), BF16), pltpu.VMEM((HEADS * ROWS, 2 * D), BF16)],
        grid=(1,),
        in_specs=[
            pl.BlockSpec(memory_space=pltpu.SMEM),
            whole(HEADS, SLOTS, D),
            pl.BlockSpec((HEADS, 32, D), lambda i: (0, ROWS // 32, 0)),
            whole(NEAR // 2, HEADS, 2, SLOTS, D),
            whole(NEAR // 2, HEADS, 2, SLOTS, D),
            whole(GROUPS, 2, 32, D),
            whole(3, HEADS, SLOTS, D),
            pl.BlockSpec(memory_space=pl.ANY),
        ],
        out_specs=[whole(HEADS, SLOTS, D), whole(NEAR, HEADS, 8, D)],
        aliases={7: 0},
        flops=1 << 30,
    )
    third = third.reshape(NEAR * HEADS, 8, D)
    third = lax.all_to_all(third, ("outer", "inner"), 0, 0, tiled=True, axis_index_groups=wide)
    o = lax.all_to_all(o, "inner", 0, 0, tiled=True)
    return call(finish, [((ROWS, HEADS * D), BF16)], (o, third))


def solution(mesh):
    rows = P(("outer", "inner"), None)
    return jax.shard_map(body, mesh=mesh, in_specs=(rows, rows, rows), out_specs=rows, check_vma=False)
```

```python
import functools
import math

import jax
import jax.numpy as jnp
from jax import lax
from jax.experimental import pallas as pl
from jax.experimental.pallas import tpu as pltpu
from jax.sharding import PartitionSpec as P

D = 128
HEADS = 8
ROWS = 256
SLOTS = 32
FAR = 4
NEAR = 8
GROUPS = 8
SCALE = D**-0.5 * math.log2(math.e)
LIMIT = 48 << 20

NT = (((1,), (1,)), ((), ()))
F32 = jnp.float32
BF16 = jnp.bfloat16


def place(t, head):
    u = t >> 3
    return (((t - head) & 7) << 5) + ((u & 7) << 2) + (u >> 3)


def to_order(head):
    p = lax.broadcasted_iota(jnp.int32, (ROWS, ROWS), 0)
    t = lax.broadcasted_iota(jnp.int32, (1, ROWS), 1)
    return jnp.where(p == place(t, head), 1.0, 0.0).astype(BF16)


def from_order(head):
    p = lax.broadcasted_iota(jnp.int32, (ROWS, ROWS), 1)
    t = lax.broadcasted_iota(jnp.int32, (ROWS, 1), 0)
    return jnp.where(p == place(t, head), 1.0, 0.0).astype(BF16)


def dot(a, b):
    return jnp.dot(a, b, preferred_element_type=F32)


def split_heads(q_hbm, k_hbm, v_hbm, qkv_ref, near_ref, q_scr, k_scr, v_scr, sems):
    pairs = ((k_hbm, k_scr), (v_hbm, v_scr), (q_hbm, q_scr))
    copies = [pltpu.make_async_copy(src, dst, sems.at[i]) for i, (src, dst) in enumerate(pairs)]
    for c in copies:
        c.start()
    for c in copies:
        c.wait()
    for h in range(HEADS):
        cols = slice(h * D, (h + 1) * D)
        rows = jnp.concatenate([k_scr[:, cols], v_scr[:, cols], q_scr[:, cols]], axis=1)
        out = dot(to_order(h), rows).astype(BF16)
        for i in range(3):
            qkv_ref[h, i] = out[:, i * D : (i + 1) * D]
        for m in range(NEAR // 2):
            near_ref[m, h, :SLOTS] = out[:SLOTS, :D]
            near_ref[m, h, SLOTS : 2 * SLOTS] = out[:SLOTS, D : 2 * D]
            near_ref[m, h, 2 * SLOTS :] = out[:16, 2 * D :]


def pick_far(here_ref, there_ref, far_ref):
    a = lax.broadcasted_iota(jnp.int32, (HEADS * FAR, ROWS), 0)
    b = lax.broadcasted_iota(jnp.int32, (HEADS * FAR, ROWS), 1)
    pick = jnp.where(b == ((a >> 2) << 5) + (a & 3), 1.0, 0.0).astype(BF16)
    for i, ref in enumerate((here_ref, there_ref)):
        for m in range(NEAR // 2):
            k2 = ref[m, :, :SLOTS].reshape(ROWS, D)
            v2 = ref[m, :, SLOTS : 2 * SLOTS].reshape(ROWS, D)
            got = dot(pick, jnp.concatenate([k2, v2], axis=1)).astype(BF16)
            at = (i * (NEAR // 2) + m) * 32
            far_ref[0, at : at + 32] = got[:, :D]
            far_ref[1, at : at + 32] = got[:, D:]


def two_parts(q):
    scaled = q.astype(F32) * SCALE
    high = scaled.astype(BF16)
    low = (scaled - high.astype(F32)).astype(BF16)
    return jnp.concatenate([high, low], axis=1)


def twice(k):
    return jnp.concatenate([k, k], axis=1)


def with_ones(v):
    return jnp.concatenate([v, jnp.ones_like(v)], axis=1)


def attend(q, keys, values):
    s = lax.dot_general(q, keys, NT, preferred_element_type=F32)
    top = jnp.max(s, axis=1, keepdims=True)
    w = jnp.exp2(s - top).astype(BF16)
    o = dot(w, values)
    return jnp.broadcast_to(top, (q.shape[0], D)), o[:, D:], o[:, :D]


def first_level(qkv_ref, o_ref, stat_ref, k_scr, v_scr):
    for s in range(HEADS):
        rows = slice(s * ROWS, (s + 1) * ROWS)
        k_scr[rows, :] = twice(qkv_ref[s, 0])
        v_scr[rows, :] = with_ones(qkv_ref[s, 1])

    def step(s, _):
        top, total, part = attend(two_parts(qkv_ref[s, 2]), k_scr[...], v_scr[...])
        o_ref[s] = (part / total).astype(BF16)
        stat_ref[0, s] = top[:SLOTS]
        stat_ref[1, s] = total[:SLOTS]
        stat_ref[2, s] = part[:SLOTS]
        return 0

    lax.fori_loop(0, HEADS, step, 0)


def merge(top_a, total_a, part_a, top_b, total_b, part_b):
    peak = jnp.maximum(top_a, top_b)
    a, b = jnp.exp2(top_a - peak), jnp.exp2(top_b - peak)
    return peak, a * total_a + b * total_b, a * part_a + b * part_b


def later_levels(own_ref, q_ref, here_ref, there_ref, far_ref, stat_ref, o_in, o_ref, third_ref, k_scr, v_scr):
    half = NEAR // 2
    for i, ref in enumerate((here_ref, there_ref)):
        for m in range(half):
            at = (i * half + m) * ROWS
            k_scr[at : at + ROWS, :] = twice(ref[m, :, :SLOTS].reshape(ROWS, D))
            v_scr[at : at + ROWS, :] = with_ones(ref[m, :, SLOTS : 2 * SLOTS].reshape(ROWS, D))
    q = two_parts(q_ref[...].reshape(ROWS, D))
    level2 = attend(q, k_scr[...], v_scr[...])
    first = [stat_ref[i].reshape(ROWS, D) for i in range(3)]
    top, total, part = merge(*first, *level2)
    o_ref[...] = (part / total).astype(BF16).reshape(HEADS, SLOTS, D)
    n = half * HEADS * 16
    a = lax.broadcasted_iota(jnp.int32, (n // 2, n), 0)
    b = lax.broadcasted_iota(jnp.int32, (n // 2, n), 1)
    pick = jnp.where(b == ((a >> 3) << 4) + (a & 3), 1.0, 0.0).astype(BF16)
    q3 = [dot(pick, ref[:, :, 2 * SLOTS :].reshape(n, D)) for ref in (here_ref, there_ref)]
    q3 = jnp.concatenate(q3, axis=0)
    level3 = attend(two_parts(q3), twice(far_ref[0]), with_ones(far_ref[1]))
    row = lax.broadcasted_iota(jnp.int32, (HEADS * 8, D), 0) & 7

    def both(x):
        x = x.reshape(HEADS, SLOTS, D)[:, :8].reshape(HEADS * 8, D)
        return jnp.where(row < 4, x, pltpu.roll(x, 4, 0))

    mine = [both(x) for x in (top, total, part)]
    core = own_ref[1]
    for j in range(NEAR):
        third = [x[j * 64 : (j + 1) * 64] for x in level3]
        if j < half:
            merged = merge(*mine, *third)
            third = [jnp.where(own_ref[0] == j, x, y) for x, y in zip(merged, third)]
        t, l, o = third
        at = 2 * j + core if j < half else 2 * (j - half) + 1 - core
        third_ref[at] = jnp.where(row < 4, o / l, t + jnp.log2(l)).reshape(HEADS, 8, D)


def finish(o_ref, third_ref, out_ref):
    parts = third_ref[...].reshape(NEAR, HEADS * 8, D)
    lse = [pltpu.roll(parts[j], HEADS * 8 - 4, 0) for j in range(NEAR)]
    peak = functools.reduce(jnp.maximum, lse)
    weights = [jnp.exp2(x - peak) for x in lse]
    total = sum(weights)
    merged = sum(w * parts[j] for j, w in enumerate(weights)) / total
    merged = merged.reshape(HEADS, 8, D)
    row = lax.broadcasted_iota(jnp.int32, (16, D), 0)
    for h in range(HEADS):
        head = o_ref[h]
        fixed = jnp.concatenate([merged[h], merged[h]], axis=0).astype(BF16)
        start = jnp.where(row < FAR, fixed, head[:16])
        head = jnp.concatenate([start, head[16:]], axis=0)
        out_ref[:, h * D : (h + 1) * D] = dot(from_order(h), head).astype(BF16)


def vmem(n):
    return [pl.BlockSpec(memory_space=pltpu.VMEM)] * n


def call(kernel, outs, ins, scratch=(), in_specs=None, out_specs=None, aliases=None, flops=0, grid=None):
    shapes = [jax.ShapeDtypeStruct(s, d) for s, d in outs]
    extra = {} if grid is None else {"grid": grid}
    got = pl.pallas_call(
        kernel,
        out_shape=shapes,
        in_specs=in_specs or vmem(len(ins)),
        out_specs=out_specs or vmem(len(outs)),
        scratch_shapes=list(scratch),
        input_output_aliases=aliases or {},
        compiler_params=pltpu.CompilerParams(vmem_limit_bytes=LIMIT),
        cost_estimate=pl.CostEstimate(flops=flops, bytes_accessed=1 << 20, transcendentals=0),
        **extra,
    )(*ins)
    return got if len(outs) > 1 else got[0]


def whole(*shape):
    return pl.BlockSpec(shape, lambda i: (0,) * len(shape))


def body(queries, keys, values):
    outer = lax.axis_size("outer")
    groups = outer // NEAR
    half = NEAR // 2
    wide = [[g * NEAR * HEADS + i for i in range(NEAR * HEADS)] for g in range(groups)]
    same_core = [
        [(g * NEAR + 2 * m + c) * HEADS + i for m in range(half) for i in range(HEADS)]
        for g in range(groups)
        for c in range(2)
    ]
    place_in_group = lax.axis_index("outer") % NEAR
    own = jnp.stack([place_in_group // 2, place_in_group % 2]).astype(jnp.int32)
    everywhere = ("outer", "inner")

    qkv, near = call(
        split_heads,
        [((HEADS, 3, ROWS, D), BF16), ((half, HEADS, 80, D), BF16)],
        (queries, keys, values),
        in_specs=[pl.BlockSpec(memory_space=pltpu.HBM)] * 3,
        scratch=[pltpu.VMEM((ROWS, HEADS * D), BF16)] * 3 + [pltpu.SemaphoreType.DMA((3,))],
    )
    near = near.reshape(half * HEADS, 80, D)
    here = lax.all_to_all(near, everywhere, 0, 0, tiled=True, axis_index_groups=same_core)
    here = here.reshape(half, HEADS, 80, D)
    there = lax.ppermute(here, "outer", [(i, i ^ 1) for i in range(outer)])
    qkv = lax.all_to_all(qkv, "inner", 0, 0, tiled=True)
    far = call(pick_far, [((2, NEAR * 32, D), BF16)], (here, there))
    moves = [(g * NEAR + j, (g + j) % groups * NEAR + j) for g in range(groups) for j in range(NEAR)]
    far = lax.ppermute(far, "outer", moves)
    o, stat = call(
        first_level,
        [((HEADS, ROWS, D), BF16), ((3, HEADS, SLOTS, D), F32)],
        (qkv,),
        scratch=[pltpu.VMEM((HEADS * ROWS, 2 * D), BF16), pltpu.VMEM((HEADS * ROWS, 2 * D), BF16)],
        flops=1 << 33,
    )
    o, third = call(
        later_levels,
        [((HEADS, ROWS, D), BF16), ((NEAR, HEADS, 8, D), F32)],
        (own, qkv, here, there, far, stat, o),
        scratch=[pltpu.VMEM((HEADS * ROWS, 2 * D), BF16), pltpu.VMEM((HEADS * ROWS, 2 * D), BF16)],
        grid=(1,),
        in_specs=[
            pl.BlockSpec(memory_space=pltpu.SMEM),
            pl.BlockSpec((HEADS, 1, SLOTS, D), lambda i: (0, 2, 0, 0)),
            whole(half, HEADS, 80, D),
            whole(half, HEADS, 80, D),
            whole(2, NEAR * 32, D),
            whole(3, HEADS, SLOTS, D),
            pl.BlockSpec(memory_space=pl.ANY),
        ],
        out_specs=[whole(HEADS, SLOTS, D), whole(NEAR, HEADS, 8, D)],
        aliases={6: 0},
        flops=1 << 30,
    )
    third = third.reshape(NEAR * HEADS, 8, D)
    third = lax.all_to_all(third, everywhere, 0, 0, tiled=True, axis_index_groups=wide)
    o = lax.all_to_all(o, "inner", 0, 0, tiled=True)
    return call(finish, [((ROWS, HEADS * D), BF16)], (o, third))


def solution(mesh):
    rows = P(("outer", "inner"), None)
    return jax.shard_map(body, mesh=mesh, in_specs=(rows, rows, rows), out_specs=rows, check_vma=False)
```

```python
import functools
import math

import jax
import jax.numpy as jnp
from jax import lax
from jax.experimental import pallas as pl
from jax.experimental.pallas import tpu as pltpu
from jax.sharding import PartitionSpec as P

D = 128
HEADS = 8
ROWS = 256
SLOTS = 32
FAR = 4
NEAR = 8
GROUPS = 8
SCALE = D**-0.5 * math.log2(math.e)
LIMIT = 48 << 20

NT = (((1,), (1,)), ((), ()))
F32 = jnp.float32
BF16 = jnp.bfloat16


def place(t, head):
    u = t >> 3
    return (((t - head) & 7) << 5) + ((u & 7) << 2) + (u >> 3)


def to_order(head, places=ROWS):
    p = lax.broadcasted_iota(jnp.int32, (places, ROWS), 0)
    t = lax.broadcasted_iota(jnp.int32, (1, ROWS), 1)
    return jnp.where(p == place(t, head), 1.0, 0.0).astype(BF16)


def from_order(head):
    p = lax.broadcasted_iota(jnp.int32, (ROWS, ROWS), 1)
    t = lax.broadcasted_iota(jnp.int32, (ROWS, 1), 0)
    return jnp.where(p == place(t, head), 1.0, 0.0).astype(BF16)


def dot(a, b):
    return jnp.dot(a, b, preferred_element_type=F32)


def chosen_rows(q_hbm, k_hbm, v_hbm, near_ref, q_scr, k_scr, v_scr, sems):
    pairs = ((k_hbm, k_scr), (v_hbm, v_scr), (q_hbm, q_scr))
    copies = [pltpu.make_async_copy(src, dst, sems.at[i]) for i, (src, dst) in enumerate(pairs)]
    for c in copies:
        c.start()
    for c in copies:
        c.wait()
    for h in range(HEADS):
        cols = slice(h * D, (h + 1) * D)
        rows = jnp.concatenate([k_scr[:, cols], v_scr[:, cols], q_scr[:, cols]], axis=1)
        out = dot(to_order(h, SLOTS), rows).astype(BF16)
        for m in range(NEAR // 2):
            near_ref[m, h, :SLOTS] = out[:, :D]
            near_ref[m, h, SLOTS : 2 * SLOTS] = out[:, D : 2 * D]
            near_ref[m, h, 2 * SLOTS :] = out[:16, 2 * D :]


def split_heads(q_hbm, k_hbm, v_hbm, qkv_hbm, q_scr, k_scr, v_scr, out_scr, in_sems, out_sems):
    pairs = ((k_hbm, k_scr), (v_hbm, v_scr), (q_hbm, q_scr))
    copies = [pltpu.make_async_copy(src, dst, in_sems.at[i]) for i, (src, dst) in enumerate(pairs)]
    for c in copies:
        c.start()
    for c in copies:
        c.wait()
    written = []
    for h in range(HEADS):
        cols = slice(h * D, (h + 1) * D)
        rows = jnp.concatenate([k_scr[:, cols], v_scr[:, cols], q_scr[:, cols]], axis=1)
        out = dot(to_order(h), rows).astype(BF16)
        for i in range(3):
            out_scr[h, i] = out[:, i * D : (i + 1) * D]
        c = pltpu.make_async_copy(out_scr.at[h], qkv_hbm.at[h], out_sems.at[h])
        c.start()
        written.append(c)
    for c in written:
        c.wait()


def pick_far(here_ref, far_ref):
    a = lax.broadcasted_iota(jnp.int32, (HEADS * FAR, ROWS), 0)
    b = lax.broadcasted_iota(jnp.int32, (HEADS * FAR, ROWS), 1)
    pick = jnp.where(b == ((a >> 2) << 5) + (a & 3), 1.0, 0.0).astype(BF16)
    for m in range(NEAR // 2):
        k2 = here_ref[m, :, :SLOTS].reshape(ROWS, D)
        v2 = here_ref[m, :, SLOTS : 2 * SLOTS].reshape(ROWS, D)
        got = dot(pick, jnp.concatenate([k2, v2], axis=1)).astype(BF16)
        far_ref[0, m * 32 : (m + 1) * 32] = got[:, :D]
        far_ref[1, m * 32 : (m + 1) * 32] = got[:, D:]


def two_parts(q):
    scaled = q.astype(F32) * SCALE
    high = scaled.astype(BF16)
    low = (scaled - high.astype(F32)).astype(BF16)
    return jnp.concatenate([high, low], axis=1)


def twice(k):
    return jnp.concatenate([k, k], axis=1)


def with_ones(v):
    return jnp.concatenate([v, jnp.ones_like(v)], axis=1)


def attend(q, keys, values):
    s = lax.dot_general(q, keys, NT, preferred_element_type=F32)
    top = jnp.max(s, axis=1, keepdims=True)
    w = jnp.exp2(s - top).astype(BF16)
    o = dot(w, values)
    return jnp.broadcast_to(top, (q.shape[0], D)), o[:, D:], o[:, :D]


def merge(top_a, total_a, part_a, top_b, total_b, part_b):
    peak = jnp.maximum(top_a, top_b)
    a, b = jnp.exp2(top_a - peak), jnp.exp2(top_b - peak)
    return peak, a * total_a + b * total_b, a * part_a + b * part_b


def two_levels(qkv_ref, here_ref, there_ref, o_ref, lse_ref, k1, v1, k2, v2, s_scr, top_scr, first):
    half = NEAR // 2
    for s in range(HEADS):
        rows = slice(s * ROWS, (s + 1) * ROWS)
        k1[rows, :] = twice(qkv_ref[s, 0])
        v1[rows, :] = with_ones(qkv_ref[s, 1])

    def scores(tile):
        if tile < HEADS:
            q, keys = qkv_ref[tile, 2], k1
        else:
            q, keys = qkv_ref[:, 2, :SLOTS].reshape(ROWS, D), k2
        x = lax.dot_general(two_parts(q), keys[...], NT, preferred_element_type=F32)
        s_scr[tile % 2] = x
        top_scr[tile % 2] = jnp.broadcast_to(jnp.max(x, axis=1, keepdims=True), (ROWS, D))

    def weigh(tile):
        top = top_scr[tile % 2]
        w = jnp.exp2(s_scr[tile % 2] - top[:, :1]).astype(BF16)
        o = dot(w, (v1 if tile < HEADS else v2)[...])
        part, total = o[:, :D], o[:, D:]
        if tile < HEADS:
            o_ref[tile, SLOTS:] = (part[SLOTS:] / total[SLOTS:]).astype(BF16)
            rows = slice(tile * SLOTS, (tile + 1) * SLOTS)
            for i, x in enumerate((top, total, part)):
                first[i, rows] = x[:SLOTS]
        else:
            top, total, part = merge(first[0], first[1], first[2], top, total, part)
            o_ref[:, :SLOTS] = (part / total).astype(BF16).reshape(HEADS, SLOTS, D)
            lse_ref[...] = (top + jnp.log2(total)).reshape(HEADS, SLOTS, D)[:, :8]

    scores(0)
    for i, ref in enumerate((here_ref, there_ref)):
        for m in range(half):
            at = (i * half + m) * ROWS
            k2[at : at + ROWS, :] = twice(ref[m, :, :SLOTS].reshape(ROWS, D))
            v2[at : at + ROWS, :] = with_ones(ref[m, :, SLOTS : 2 * SLOTS].reshape(ROWS, D))
    for tile in range(HEADS + 1):
        if tile < HEADS:
            scores(tile + 1)
        weigh(tile)


def merge_third(lse_ref, third_ref, o_in, o_ref):
    o = o_in[...].astype(F32)
    base = o[:, :8].reshape(HEADS * 8, D)
    parts = [third_ref[j].reshape(HEADS * 8, D) for j in range(NEAR)]
    sums = [lse_ref[...].reshape(HEADS * 8, D)] + [pltpu.roll(x, HEADS * 8 - 4, 0) for x in parts]
    peak = functools.reduce(jnp.maximum, sums)
    weights = [jnp.exp2(x - peak) for x in sums]
    last = sum(w * x for w, x in zip(weights, [base] + parts)) / sum(weights)
    row = lax.broadcasted_iota(jnp.int32, (HEADS * 8, D), 0) & 7
    last = jnp.where(row < FAR, last, base).reshape(HEADS, 8, D)
    o_ref[...] = jnp.concatenate([last, o[:, 8:]], axis=1).astype(BF16)


def third_level(core_ref, here_ref, there_ref, far_a, far_b, third_ref):
    half = NEAR // 2
    n = half * HEADS * 16
    a = lax.broadcasted_iota(jnp.int32, (n // 2, n), 0)
    b = lax.broadcasted_iota(jnp.int32, (n // 2, n), 1)
    pick = jnp.where(b == ((a >> 3) << 4) + (a & 3), 1.0, 0.0).astype(BF16)
    q3 = [dot(pick, ref[:, :, 2 * SLOTS :].reshape(n, D)) for ref in (here_ref, there_ref)]
    q3 = jnp.concatenate(q3, axis=0)
    k3 = jnp.concatenate([far_a[0], far_b[0]], axis=0)
    v3 = jnp.concatenate([far_a[1], far_b[1]], axis=0)
    level3 = attend(two_parts(q3), twice(k3), with_ones(v3))
    row = lax.broadcasted_iota(jnp.int32, (HEADS * 8, D), 0) & 7
    core = core_ref[0]
    for j in range(NEAR):
        t, l, o = [x[j * 64 : (j + 1) * 64] for x in level3]
        at = 2 * j + core if j < half else 2 * (j - half) + 1 - core
        third_ref[at] = jnp.where(row < 4, o / l, t + jnp.log2(l)).reshape(HEADS, 8, D)


def finish(o_ref, out_ref):
    for h in range(HEADS):
        out_ref[:, h * D : (h + 1) * D] = dot(from_order(h), o_ref[h]).astype(BF16)


def vmem(n):
    return [pl.BlockSpec(memory_space=pltpu.VMEM)] * n


def call(kernel, outs, ins, scratch=(), in_specs=None, out_specs=None, aliases=None, flops=0, grid=None, limit=LIMIT):
    shapes = [jax.ShapeDtypeStruct(s, d) for s, d in outs]
    extra = {} if grid is None else {"grid": grid}
    got = pl.pallas_call(
        kernel,
        out_shape=shapes,
        in_specs=in_specs or vmem(len(ins)),
        out_specs=out_specs or vmem(len(outs)),
        scratch_shapes=list(scratch),
        input_output_aliases=aliases or {},
        compiler_params=pltpu.CompilerParams(vmem_limit_bytes=limit),
        cost_estimate=pl.CostEstimate(flops=flops, bytes_accessed=1 << 20, transcendentals=0),
        **extra,
    )(*ins)
    return got if len(outs) > 1 else got[0]


def whole(*shape):
    return pl.BlockSpec(shape, lambda i: (0,) * len(shape))


def body(queries, keys, values):
    outer = lax.axis_size("outer")
    groups = outer // NEAR
    half = NEAR // 2
    near_groups = [[g * NEAR + j for j in range(NEAR)] for g in range(groups)]
    same_core = [
        [(g * NEAR + 2 * m + c) * HEADS + i for m in range(half) for i in range(HEADS)]
        for g in range(groups)
        for c in range(2)
    ]
    core = (lax.axis_index("outer") % 2).astype(jnp.int32).reshape(1)
    anywhere = pl.BlockSpec(memory_space=pl.ANY)
    block = pltpu.VMEM((ROWS, HEADS * D), BF16)

    near = call(
        chosen_rows,
        [((half, HEADS, 80, D), BF16)],
        (queries, keys, values),
        in_specs=[anywhere] * 3,
        scratch=[block] * 3 + [pltpu.SemaphoreType.DMA((3,))],
        limit=60 << 20,
    )
    near = near.reshape(half * HEADS, 80, D)
    here = lax.all_to_all(near, ("outer", "inner"), 0, 0, tiled=True, axis_index_groups=same_core)
    here = here.reshape(half, HEADS, 80, D)
    there = lax.ppermute(here, "outer", [(i, i ^ 1) for i in range(outer)])
    qkv = call(
        split_heads,
        [((HEADS, 3, ROWS, D), BF16)],
        (queries, keys, values),
        in_specs=[anywhere] * 3,
        out_specs=[anywhere],
        scratch=[block] * 3
        + [pltpu.VMEM((HEADS, 3, ROWS, D), BF16), pltpu.SemaphoreType.DMA((3,)), pltpu.SemaphoreType.DMA((HEADS,))],
        limit=60 << 20,
    )
    qkv = lax.all_to_all(qkv, "inner", 0, 0, tiled=True)
    far = call(pick_far, [((2, half * 32, D), BF16)], (here,))
    place = [(g, j) for g in range(groups) for j in range(NEAR)]
    far_a, far_b = [
        lax.ppermute(far, "outer", [(g * NEAR + j, (g + j // 2 + by) % groups * NEAR + j) for g, j in place])
        for by in (0, groups // 2)
    ]
    third = call(
        third_level,
        [((NEAR, HEADS, 8, D), F32)],
        (core, here, there, far_a, far_b),
        in_specs=[pl.BlockSpec(memory_space=pltpu.SMEM)] + vmem(4),
        flops=1 << 28,
    )
    third = lax.all_to_all(third, "outer", 0, 0, tiled=True, axis_index_groups=near_groups)
    o, lse = call(
        two_levels,
        [((HEADS, ROWS, D), BF16), ((HEADS, 8, D), F32)],
        (qkv, here, there),
        scratch=[pltpu.VMEM((HEADS * ROWS, 2 * D), BF16)] * 4
        + [pltpu.VMEM((2, ROWS, HEADS * ROWS), F32), pltpu.VMEM((2, ROWS, D), F32), pltpu.VMEM((3, ROWS, D), F32)],
        flops=1 << 33,
    )
    o = call(
        merge_third,
        [((HEADS, ROWS, D), BF16)],
        (lse, third, o),
        grid=(1,),
        in_specs=[whole(HEADS, 8, D), whole(NEAR, HEADS, 8, D), whole(HEADS, 16, D)],
        out_specs=[whole(HEADS, 16, D)],
        aliases={2: 0},
    )
    o = lax.all_to_all(o, "inner", 0, 0, tiled=True)
    return call(finish, [((ROWS, HEADS * D), BF16)], (o,))


def solution(mesh):
    rows = P(("outer", "inner"), None)
    return jax.shard_map(body, mesh=mesh, in_specs=(rows, rows, rows), out_specs=rows, check_vma=False)
```

```python
import functools
import math

import jax
import jax.numpy as jnp
from jax import lax
from jax.experimental import pallas as pl
from jax.experimental.pallas import tpu as pltpu
from jax.sharding import PartitionSpec as P

D = 128
HEADS = 8
ROWS = 256
SLOTS = 32
FAR = 4
NEAR = 8
GROUPS = 8
SCALE = D**-0.5 * math.log2(math.e)
LIMIT = 48 << 20

NT = (((1,), (1,)), ((), ()))
F32 = jnp.float32
BF16 = jnp.bfloat16


def place(t, head):
    u = t >> 3
    return (((t - head) & 7) << 5) + ((u & 7) << 2) + (u >> 3)


def to_order(head, places=ROWS):
    p = lax.broadcasted_iota(jnp.int32, (places, ROWS), 0)
    t = lax.broadcasted_iota(jnp.int32, (1, ROWS), 1)
    return jnp.where(p == place(t, head), 1.0, 0.0).astype(BF16)


def from_order(head):
    p = lax.broadcasted_iota(jnp.int32, (ROWS, ROWS), 1)
    t = lax.broadcasted_iota(jnp.int32, (ROWS, 1), 0)
    return jnp.where(p == place(t, head), 1.0, 0.0).astype(BF16)


def dot(a, b):
    return jnp.dot(a, b, preferred_element_type=F32)


def chosen_rows(q_hbm, k_hbm, v_hbm, near_ref, q_scr, k_scr, v_scr, sems):
    pairs = ((k_hbm, k_scr), (v_hbm, v_scr), (q_hbm, q_scr))
    copies = [pltpu.make_async_copy(src, dst, sems.at[i]) for i, (src, dst) in enumerate(pairs)]
    for c in copies:
        c.start()
    for c in copies:
        c.wait()
    for h in range(HEADS):
        cols = slice(h * D, (h + 1) * D)
        rows = jnp.concatenate([k_scr[:, cols], v_scr[:, cols], q_scr[:, cols]], axis=1)
        out = dot(to_order(h, SLOTS), rows).astype(BF16)
        for m in range(NEAR // 2):
            near_ref[m, h, :SLOTS] = out[:, :D]
            near_ref[m, h, SLOTS : 2 * SLOTS] = out[:, D : 2 * D]
            near_ref[m, h, 2 * SLOTS :] = out[:16, 2 * D :]


def split_heads(q_hbm, k_hbm, v_hbm, qkv_hbm, q_scr, k_scr, v_scr, out_scr, in_sems, out_sems):
    pairs = ((k_hbm, k_scr), (v_hbm, v_scr), (q_hbm, q_scr))
    copies = [pltpu.make_async_copy(src, dst, in_sems.at[i]) for i, (src, dst) in enumerate(pairs)]
    for c in copies:
        c.start()
    for c in copies:
        c.wait()
    written = []
    for h in range(HEADS):
        cols = slice(h * D, (h + 1) * D)
        rows = jnp.concatenate([k_scr[:, cols], v_scr[:, cols], q_scr[:, cols]], axis=1)
        out = dot(to_order(h), rows).astype(BF16)
        for i in range(3):
            out_scr[h, i] = out[:, i * D : (i + 1) * D]
        c = pltpu.make_async_copy(out_scr.at[h], qkv_hbm.at[h], out_sems.at[h])
        c.start()
        written.append(c)
    for c in written:
        c.wait()


def pick_chosen(near_ref, far_ref, q3_ref, kv_ref):
    kv_ref[...] = near_ref[:, :, : 2 * SLOTS]
    a = lax.broadcasted_iota(jnp.int32, (HEADS * FAR, ROWS), 0)
    b = lax.broadcasted_iota(jnp.int32, (HEADS * FAR, ROWS), 1)
    pick = jnp.where(b == ((a >> 2) << 5) + (a & 3), 1.0, 0.0).astype(BF16)
    pick16 = jnp.where(b[:, : ROWS // 2] == ((a[:, : ROWS // 2] >> 2) << 4) + (a[:, : ROWS // 2] & 3), 1.0, 0.0)
    pick16 = pick16.astype(BF16)
    for m in range(NEAR // 2):
        k2 = near_ref[m, :, :SLOTS].reshape(ROWS, D)
        v2 = near_ref[m, :, SLOTS : 2 * SLOTS].reshape(ROWS, D)
        got = dot(pick, jnp.concatenate([k2, v2], axis=1)).astype(BF16)
        far_ref[0, m * 32 : (m + 1) * 32] = got[:, :D]
        far_ref[1, m * 32 : (m + 1) * 32] = got[:, D:]
        q = near_ref[m, :, 2 * SLOTS :].reshape(HEADS * 16, D)
        q3_ref[m * 32 : (m + 1) * 32] = dot(pick16, q).astype(BF16)


def two_parts(q):
    scaled = q.astype(F32) * SCALE
    high = scaled.astype(BF16)
    low = (scaled - high.astype(F32)).astype(BF16)
    return jnp.concatenate([high, low], axis=1)


def twice(k):
    return jnp.concatenate([k, k], axis=1)


def with_ones(v):
    return jnp.concatenate([v, jnp.ones_like(v)], axis=1)


def attend(q, keys, values):
    s = lax.dot_general(q, keys, NT, preferred_element_type=F32)
    top = jnp.max(s, axis=1, keepdims=True)
    w = jnp.exp2(s - top).astype(BF16)
    o = dot(w, values)
    return jnp.broadcast_to(top, (q.shape[0], D)), o[:, D:], o[:, :D]


def merge(top_a, total_a, part_a, top_b, total_b, part_b):
    peak = jnp.maximum(top_a, top_b)
    a, b = jnp.exp2(top_a - peak), jnp.exp2(top_b - peak)
    return peak, a * total_a + b * total_b, a * part_a + b * part_b


def two_levels(qkv_ref, here_ref, there_hbm, o_ref, lse_ref, k1, v1, k2, v2, s_scr, top_scr, first, there_ref, sem):
    fetch = pltpu.make_async_copy(there_hbm, there_ref, sem)
    fetch.start()
    half = NEAR // 2
    for s in range(HEADS):
        rows = slice(s * ROWS, (s + 1) * ROWS)
        k1[rows, :] = twice(qkv_ref[s, 0])
        v1[rows, :] = with_ones(qkv_ref[s, 1])

    def scores(tile):
        if tile < HEADS:
            q, keys = qkv_ref[tile, 2], k1
        else:
            q, keys = qkv_ref[:, 2, :SLOTS].reshape(ROWS, D), k2
        x = lax.dot_general(two_parts(q), keys[...], NT, preferred_element_type=F32)
        s_scr[tile % 2] = x
        top_scr[tile % 2] = jnp.broadcast_to(jnp.max(x, axis=1, keepdims=True), (ROWS, D))

    def weigh(tile):
        top = top_scr[tile % 2]
        w = jnp.exp2(s_scr[tile % 2] - top[:, :1]).astype(BF16)
        o = dot(w, (v1 if tile < HEADS else v2)[...])
        part, total = o[:, :D], o[:, D:]
        if tile < HEADS:
            o_ref[tile, SLOTS:] = (part[SLOTS:] / total[SLOTS:]).astype(BF16)
            rows = slice(tile * SLOTS, (tile + 1) * SLOTS)
            for i, x in enumerate((top, total, part)):
                first[i, rows] = x[:SLOTS]
        else:
            top, total, part = merge(first[0], first[1], first[2], top, total, part)
            o_ref[:, :SLOTS] = (part / total).astype(BF16).reshape(HEADS, SLOTS, D)
            lse_ref[...] = (top + jnp.log2(total)).reshape(HEADS, SLOTS, D)[:, :8]

    scores(0)
    fetch.wait()
    for i, ref in enumerate((here_ref, there_ref)):
        for m in range(half):
            at = (i * half + m) * ROWS
            k2[at : at + ROWS, :] = twice(ref[m, :, :SLOTS].reshape(ROWS, D))
            v2[at : at + ROWS, :] = with_ones(ref[m, :, SLOTS : 2 * SLOTS].reshape(ROWS, D))
    for tile in range(HEADS + 1):
        if tile < HEADS:
            scores(tile + 1)
        weigh(tile)


def merge_third(lse_ref, third_ref, o_in, o_ref):
    o = o_in[...].astype(F32)
    base = o[:, :8].reshape(HEADS * 8, D)
    parts = [third_ref[j].reshape(HEADS * 8, D) for j in range(NEAR)]
    sums = [lse_ref[...].reshape(HEADS * 8, D)] + [pltpu.roll(x, HEADS * 8 - 4, 0) for x in parts]
    peak = functools.reduce(jnp.maximum, sums)
    weights = [jnp.exp2(x - peak) for x in sums]
    last = sum(w * x for w, x in zip(weights, [base] + parts)) / sum(weights)
    row = lax.broadcasted_iota(jnp.int32, (HEADS * 8, D), 0) & 7
    last = jnp.where(row < FAR, last, base).reshape(HEADS, 8, D)
    o_ref[...] = jnp.concatenate([last, o[:, 8:]], axis=1).astype(BF16)


def third_level(core_ref, here_ref, there_ref, far_a, far_b, third_ref):
    half = NEAR // 2
    n = half * HEADS * FAR
    a = lax.broadcasted_iota(jnp.int32, (2 * n, n), 0)
    b = lax.broadcasted_iota(jnp.int32, (2 * n, n), 1)
    pick = jnp.where(b == ((a >> 3) << 2) + (a & 3), 1.0, 0.0).astype(BF16)
    q3 = jnp.concatenate([dot(pick, here_ref[...]), dot(pick, there_ref[...])], axis=0).astype(BF16)
    k3 = jnp.concatenate([far_a[0], far_b[0]], axis=0)
    v3 = jnp.concatenate([far_a[1], far_b[1]], axis=0)
    level3 = attend(two_parts(q3), twice(k3), with_ones(v3))
    row = lax.broadcasted_iota(jnp.int32, (HEADS * 8, D), 0) & 7
    core = core_ref[0]
    for j in range(NEAR):
        t, l, o = [x[j * 64 : (j + 1) * 64] for x in level3]
        at = 2 * j + core if j < half else 2 * (j - half) + 1 - core
        third_ref[at] = jnp.where(row < 4, o / l, t + jnp.log2(l)).reshape(HEADS, 8, D)


def finish(o_ref, out_ref):
    for h in range(HEADS):
        out_ref[:, h * D : (h + 1) * D] = dot(from_order(h), o_ref[h]).astype(BF16)


def vmem(n):
    return [pl.BlockSpec(memory_space=pltpu.VMEM)] * n


def call(kernel, outs, ins, scratch=(), in_specs=None, out_specs=None, aliases=None, flops=0, grid=None, limit=LIMIT):
    shapes = [jax.ShapeDtypeStruct(s, d) for s, d in outs]
    extra = {} if grid is None else {"grid": grid}
    got = pl.pallas_call(
        kernel,
        out_shape=shapes,
        in_specs=in_specs or vmem(len(ins)),
        out_specs=out_specs or vmem(len(outs)),
        scratch_shapes=list(scratch),
        input_output_aliases=aliases or {},
        compiler_params=pltpu.CompilerParams(vmem_limit_bytes=limit),
        cost_estimate=pl.CostEstimate(flops=flops, bytes_accessed=1 << 20, transcendentals=0),
        **extra,
    )(*ins)
    return got if len(outs) > 1 else got[0]


def whole(*shape):
    return pl.BlockSpec(shape, lambda i: (0,) * len(shape))


def body(queries, keys, values):
    outer = lax.axis_size("outer")
    groups = outer // NEAR
    half = NEAR // 2
    near_groups = [[g * NEAR + j for j in range(NEAR)] for g in range(groups)]
    same_core = [
        [(g * NEAR + 2 * m + c) * HEADS + i for m in range(half) for i in range(HEADS)]
        for g in range(groups)
        for c in range(2)
    ]
    core = (lax.axis_index("outer") % 2).astype(jnp.int32).reshape(1)
    anywhere = pl.BlockSpec(memory_space=pl.ANY)
    block = pltpu.VMEM((ROWS, HEADS * D), BF16)

    near = call(
        chosen_rows,
        [((half, HEADS, 80, D), BF16)],
        (queries, keys, values),
        in_specs=[anywhere] * 3,
        scratch=[block] * 3 + [pltpu.SemaphoreType.DMA((3,))],
        limit=60 << 20,
    )
    near = near.reshape(half * HEADS, 80, D)
    here = lax.all_to_all(near, ("outer", "inner"), 0, 0, tiled=True, axis_index_groups=same_core)
    here = here.reshape(half, HEADS, 80, D)
    qkv = call(
        split_heads,
        [((HEADS, 3, ROWS, D), BF16)],
        (queries, keys, values),
        in_specs=[anywhere] * 3,
        out_specs=[anywhere],
        scratch=[block] * 3
        + [pltpu.VMEM((HEADS, 3, ROWS, D), BF16), pltpu.SemaphoreType.DMA((3,)), pltpu.SemaphoreType.DMA((HEADS,))],
        limit=60 << 20,
    )
    qkv = lax.all_to_all(qkv, "inner", 0, 0, tiled=True)
    far, q3_here, here = call(
        pick_chosen,
        [((2, half * 32, D), BF16), ((half * 32, D), BF16), ((half, HEADS, 2 * SLOTS, D), BF16)],
        (here,),
    )
    other_core = [(i, i ^ 1) for i in range(outer)]
    place = [(g, j) for g in range(groups) for j in range(NEAR)]
    far_a, far_b = [
        lax.ppermute(far, "outer", [(g * NEAR + j, (g + by[j // 2]) % groups * NEAR + j) for g, j in place])
        for by in ((4, 1, 2, 3), (0, 5, 6, 7))
    ]
    q3_there = lax.ppermute(q3_here, "outer", other_core)
    there = lax.ppermute(here, "outer", other_core)
    third = call(
        third_level,
        [((NEAR, HEADS, 8, D), F32)],
        (core, q3_here, q3_there, far_a, far_b),
        in_specs=[pl.BlockSpec(memory_space=pltpu.SMEM)] + vmem(4),
        flops=1 << 32,
    )
    third = lax.all_to_all(third, "outer", 0, 0, tiled=True, axis_index_groups=near_groups)
    o, lse = call(
        two_levels,
        [((HEADS, ROWS, D), BF16), ((HEADS, 8, D), F32)],
        (qkv, here, there),
        in_specs=vmem(2) + [anywhere],
        scratch=[pltpu.VMEM((HEADS * ROWS, 2 * D), BF16)] * 4
        + [pltpu.VMEM((2, ROWS, HEADS * ROWS), F32), pltpu.VMEM((2, ROWS, D), F32), pltpu.VMEM((3, ROWS, D), F32)]
        + [pltpu.VMEM((half, HEADS, 2 * SLOTS, D), BF16), pltpu.SemaphoreType.DMA],
        flops=1 << 33,
    )
    o = call(
        merge_third,
        [((HEADS, ROWS, D), BF16)],
        (lse, third, o),
        grid=(1,),
        in_specs=[whole(HEADS, 8, D), whole(NEAR, HEADS, 8, D), whole(HEADS, 16, D)],
        out_specs=[whole(HEADS, 16, D)],
        aliases={2: 0},
    )
    o = lax.all_to_all(o, "inner", 0, 0, tiled=True)
    return call(finish, [((ROWS, HEADS * D), BF16)], (o,))


def solution(mesh):
    rows = P(("outer", "inner"), None)
    return jax.shard_map(body, mesh=mesh, in_specs=(rows, rows, rows), out_specs=rows, check_vma=False)
```

```python
import functools
import math

import jax
import jax.numpy as jnp
from jax import lax
from jax.experimental import pallas as pl
from jax.experimental.pallas import tpu as pltpu
from jax.sharding import PartitionSpec as P

D = 128
HEADS = 8
ROWS = 256
SLOTS = 32
FAR = 4
NEAR = 8
GROUPS = 8
SCALE = D**-0.5 * math.log2(math.e)
LIMIT = 48 << 20

NT = (((1,), (1,)), ((), ()))
F32 = jnp.float32
BF16 = jnp.bfloat16


def place(t, head):
    u = t >> 3
    return (((t - head) & 7) << 5) + ((u & 7) << 2) + (u >> 3)


def to_order(head, places=ROWS):
    p = lax.broadcasted_iota(jnp.int32, (places, ROWS), 0)
    t = lax.broadcasted_iota(jnp.int32, (1, ROWS), 1)
    return jnp.where(p == place(t, head), 1.0, 0.0).astype(BF16)


def from_order(head):
    p = lax.broadcasted_iota(jnp.int32, (ROWS, ROWS), 1)
    t = lax.broadcasted_iota(jnp.int32, (ROWS, 1), 0)
    return jnp.where(p == place(t, head), 1.0, 0.0).astype(BF16)


def dot(a, b):
    return jnp.dot(a, b, preferred_element_type=F32)


def chosen_rows(q_hbm, k_hbm, v_hbm, near_hbm, q_scr, k_scr, v_scr, out_scr, in_sems, out_sems):
    copies = [pltpu.make_async_copy(k_hbm, k_scr, in_sems.at[0]), pltpu.make_async_copy(v_hbm, v_scr, in_sems.at[1])]
    copies += [
        pltpu.make_async_copy(q_hbm.at[pl.ds(64 * s, 8)], q_scr.at[pl.ds(8 * s, 8)], in_sems.at[2 + s])
        for s in range(FAR)
    ]
    for c in copies:
        c.start()
    written = []

    def send(i, at, rows):
        part = (slice(None), pl.ds(at, rows))
        for m in range(NEAR // 2):
            c = pltpu.make_async_copy(out_scr.at[part], near_hbm.at[(m, *part)], out_sems.at[i, m])
            c.start()
            written.append(c)

    for i, scr in enumerate((k_scr, v_scr)):
        copies[i].wait()
        for h in range(HEADS):
            got = dot(to_order(h, SLOTS), scr[:, h * D : (h + 1) * D])
            out_scr[h, i * SLOTS : (i + 1) * SLOTS] = got.astype(BF16)
        send(i, i * SLOTS, SLOTS)
    for c in copies[2:]:
        c.wait()
    slot = lax.broadcasted_iota(jnp.int32, (16, 8 * FAR), 0)
    row = lax.broadcasted_iota(jnp.int32, (16, 8 * FAR), 1)
    for h in range(HEADS):
        pick = jnp.where((row == 8 * slot + h) & (slot < FAR), 1.0, 0.0).astype(BF16)
        out_scr[h, 2 * SLOTS :] = dot(pick, q_scr[:, h * D : (h + 1) * D]).astype(BF16)
    send(2, 2 * SLOTS, 16)
    for c in written:
        c.wait()


def split_heads(q_hbm, k_hbm, v_hbm, qkv_hbm, q_scr, k_scr, v_scr, out_scr, in_sems, out_sems):
    pairs = ((k_hbm, k_scr), (v_hbm, v_scr), (q_hbm, q_scr))
    copies = [pltpu.make_async_copy(src, dst, in_sems.at[i]) for i, (src, dst) in enumerate(pairs)]
    for c in copies:
        c.start()
    for c in copies:
        c.wait()
    written = []
    for h in range(HEADS):
        cols = slice(h * D, (h + 1) * D)
        rows = jnp.concatenate([k_scr[:, cols], v_scr[:, cols], q_scr[:, cols]], axis=1)
        out = dot(to_order(h), rows).astype(BF16)
        for i in range(3):
            out_scr[h, i] = out[:, i * D : (i + 1) * D]
        c = pltpu.make_async_copy(out_scr.at[h], qkv_hbm.at[h], out_sems.at[h])
        c.start()
        written.append(c)
    for c in written:
        c.wait()


def pick_chosen(near_ref, far_ref, q3_ref, kv_ref):
    kv_ref[...] = near_ref[:, :, : 2 * SLOTS]
    a = lax.broadcasted_iota(jnp.int32, (HEADS * FAR, ROWS), 0)
    b = lax.broadcasted_iota(jnp.int32, (HEADS * FAR, ROWS), 1)
    pick = jnp.where(b == ((a >> 2) << 5) + (a & 3), 1.0, 0.0).astype(BF16)
    pick16 = jnp.where(b[:, : ROWS // 2] == ((a[:, : ROWS // 2] >> 2) << 4) + (a[:, : ROWS // 2] & 3), 1.0, 0.0)
    pick16 = pick16.astype(BF16)
    for m in range(NEAR // 2):
        k2 = near_ref[m, :, :SLOTS].reshape(ROWS, D)
        v2 = near_ref[m, :, SLOTS : 2 * SLOTS].reshape(ROWS, D)
        got = dot(pick, jnp.concatenate([k2, v2], axis=1)).astype(BF16)
        far_ref[0, m * 32 : (m + 1) * 32] = got[:, :D]
        far_ref[1, m * 32 : (m + 1) * 32] = got[:, D:]
        q = near_ref[m, :, 2 * SLOTS :].reshape(HEADS * 16, D)
        q3_ref[m * 32 : (m + 1) * 32] = dot(pick16, q).astype(BF16)


def two_parts(q):
    scaled = q.astype(F32) * SCALE
    high = scaled.astype(BF16)
    low = (scaled - high.astype(F32)).astype(BF16)
    return jnp.concatenate([high, low], axis=1)


def twice(k):
    return jnp.concatenate([k, k], axis=1)


def with_ones(v):
    return jnp.concatenate([v, jnp.ones_like(v)], axis=1)


def attend(q, keys, values):
    s = lax.dot_general(q, keys, NT, preferred_element_type=F32)
    top = jnp.max(s, axis=1, keepdims=True)
    w = jnp.exp2(s - top).astype(BF16)
    o = dot(w, values)
    return jnp.broadcast_to(top, (q.shape[0], D)), o[:, D:], o[:, :D]


def merge(top_a, total_a, part_a, top_b, total_b, part_b):
    peak = jnp.maximum(top_a, top_b)
    a, b = jnp.exp2(top_a - peak), jnp.exp2(top_b - peak)
    return peak, a * total_a + b * total_b, a * part_a + b * part_b


def two_levels(qkv_ref, here_ref, there_hbm, o_ref, lse_ref, k1, v1, k2, v2, s_scr, top_scr, first, there_ref, sem):
    fetch = pltpu.make_async_copy(there_hbm, there_ref, sem)
    fetch.start()
    half = NEAR // 2
    for s in range(HEADS):
        rows = slice(s * ROWS, (s + 1) * ROWS)
        k1[rows, :] = twice(qkv_ref[s, 0])
        v1[rows, :] = with_ones(qkv_ref[s, 1])

    def scores(tile):
        if tile < HEADS:
            q, keys = qkv_ref[tile, 2], k1
        else:
            q, keys = qkv_ref[:, 2, :SLOTS].reshape(ROWS, D), k2
        x = lax.dot_general(two_parts(q), keys[...], NT, preferred_element_type=F32)
        s_scr[tile % 2] = x
        top_scr[tile % 2] = jnp.broadcast_to(jnp.max(x, axis=1, keepdims=True), (ROWS, D))

    def weigh(tile):
        top = top_scr[tile % 2]
        w = jnp.exp2(s_scr[tile % 2] - top[:, :1]).astype(BF16)
        o = dot(w, (v1 if tile < HEADS else v2)[...])
        part, total = o[:, :D], o[:, D:]
        if tile < HEADS:
            o_ref[tile, SLOTS:] = (part[SLOTS:] / total[SLOTS:]).astype(BF16)
            rows = slice(tile * SLOTS, (tile + 1) * SLOTS)
            for i, x in enumerate((top, total, part)):
                first[i, rows] = x[:SLOTS]
        else:
            top, total, part = merge(first[0], first[1], first[2], top, total, part)
            o_ref[:, :SLOTS] = (part / total).astype(BF16).reshape(HEADS, SLOTS, D)
            lse_ref[...] = (top + jnp.log2(total)).reshape(HEADS, SLOTS, D)[:, :8]

    scores(0)
    fetch.wait()
    for i, ref in enumerate((here_ref, there_ref)):
        for m in range(half):
            at = (i * half + m) * ROWS
            k2[at : at + ROWS, :] = twice(ref[m, :, :SLOTS].reshape(ROWS, D))
            v2[at : at + ROWS, :] = with_ones(ref[m, :, SLOTS : 2 * SLOTS].reshape(ROWS, D))
    for tile in range(HEADS + 1):
        if tile < HEADS:
            scores(tile + 1)
        weigh(tile)


def merge_third(lse_ref, third_ref, o_in, o_ref):
    o = o_in[...].astype(F32)
    base = o[:, :8].reshape(HEADS * 8, D)
    parts = [third_ref[j].reshape(HEADS * 8, D) for j in range(NEAR)]
    sums = [lse_ref[...].reshape(HEADS * 8, D)] + [pltpu.roll(x, HEADS * 8 - 4, 0) for x in parts]
    peak = functools.reduce(jnp.maximum, sums)
    weights = [jnp.exp2(x - peak) for x in sums]
    last = sum(w * x for w, x in zip(weights, [base] + parts)) / sum(weights)
    row = lax.broadcasted_iota(jnp.int32, (HEADS * 8, D), 0) & 7
    last = jnp.where(row < FAR, last, base).reshape(HEADS, 8, D)
    o_ref[...] = jnp.concatenate([last, o[:, 8:]], axis=1).astype(BF16)


def third_level(core_ref, here_ref, there_ref, far_a, far_b, third_hbm, third_scr, sems):
    half = NEAR // 2
    n = half * HEADS * FAR
    a = lax.broadcasted_iota(jnp.int32, (2 * n, n), 0)
    b = lax.broadcasted_iota(jnp.int32, (2 * n, n), 1)
    pick = jnp.where(b == ((a >> 3) << 2) + (a & 3), 1.0, 0.0).astype(BF16)
    q3 = jnp.concatenate([dot(pick, here_ref[...]), dot(pick, there_ref[...])], axis=0).astype(BF16)
    k3 = jnp.concatenate([far_a[0], far_b[0]], axis=0)
    v3 = jnp.concatenate([far_a[1], far_b[1]], axis=0)
    level3 = attend(two_parts(q3), twice(k3), with_ones(v3))
    row = lax.broadcasted_iota(jnp.int32, (HEADS * 8, D), 0) & 7
    core = core_ref[0]
    written = []
    for j in range(NEAR):
        t, l, o = [x[j * 64 : (j + 1) * 64] for x in level3]
        at = 2 * j + core if j < half else 2 * (j - half) + 1 - core
        third_scr[j] = jnp.where(row < 4, o / l, t + jnp.log2(l)).reshape(HEADS, 8, D)
        c = pltpu.make_async_copy(third_scr.at[j], third_hbm.at[at], sems.at[j])
        c.start()
        written.append(c)
    for c in written:
        c.wait()


def finish(o_ref, out_hbm, out_scr, sems):
    orders = [from_order(h) for h in range(HEADS)]
    written = []
    for i in range(4):
        rows = slice(i * ROWS // 4, (i + 1) * ROWS // 4)
        for h in range(HEADS):
            out_scr[rows, h * D : (h + 1) * D] = dot(orders[h][rows], o_ref[h]).astype(BF16)
        c = pltpu.make_async_copy(out_scr.at[rows], out_hbm.at[rows], sems.at[i])
        c.start()
        written.append(c)
    for c in written:
        c.wait()


def vmem(n):
    return [pl.BlockSpec(memory_space=pltpu.VMEM)] * n


def call(kernel, outs, ins, scratch=(), in_specs=None, out_specs=None, aliases=None, flops=0, grid=None, limit=LIMIT):
    shapes = [jax.ShapeDtypeStruct(s, d) for s, d in outs]
    extra = {} if grid is None else {"grid": grid}
    got = pl.pallas_call(
        kernel,
        out_shape=shapes,
        in_specs=in_specs or vmem(len(ins)),
        out_specs=out_specs or vmem(len(outs)),
        scratch_shapes=list(scratch),
        input_output_aliases=aliases or {},
        compiler_params=pltpu.CompilerParams(vmem_limit_bytes=limit),
        cost_estimate=pl.CostEstimate(flops=flops, bytes_accessed=1 << 20, transcendentals=0),
        **extra,
    )(*ins)
    return got if len(outs) > 1 else got[0]


def whole(*shape):
    return pl.BlockSpec(shape, lambda i: (0,) * len(shape))


def body(queries, keys, values):
    outer = lax.axis_size("outer")
    groups = outer // NEAR
    half = NEAR // 2
    near_groups = [[g * NEAR + j for j in range(NEAR)] for g in range(groups)]
    same_core = [
        [(g * NEAR + 2 * m + c) * HEADS + i for m in range(half) for i in range(HEADS)]
        for g in range(groups)
        for c in range(2)
    ]
    core = (lax.axis_index("outer") % 2).astype(jnp.int32).reshape(1)
    anywhere = pl.BlockSpec(memory_space=pl.ANY)
    block = pltpu.VMEM((ROWS, HEADS * D), BF16)

    near = call(
        chosen_rows,
        [((half, HEADS, 80, D), BF16)],
        (queries, keys, values),
        in_specs=[anywhere] * 3,
        out_specs=[anywhere],
        scratch=[
            pltpu.VMEM((8 * FAR, HEADS * D), BF16),
            block,
            block,
            pltpu.VMEM((HEADS, 80, D), BF16),
            pltpu.SemaphoreType.DMA((2 + FAR,)),
            pltpu.SemaphoreType.DMA((3, half)),
        ],
        limit=60 << 20,
    )
    near = near.reshape(half * HEADS, 80, D)
    here = lax.all_to_all(near, ("outer", "inner"), 0, 0, tiled=True, axis_index_groups=same_core)
    here = here.reshape(half, HEADS, 80, D)
    qkv = call(
        split_heads,
        [((HEADS, 3, ROWS, D), BF16)],
        (queries, keys, values),
        in_specs=[anywhere] * 3,
        out_specs=[anywhere],
        scratch=[block] * 3
        + [pltpu.VMEM((HEADS, 3, ROWS, D), BF16), pltpu.SemaphoreType.DMA((3,)), pltpu.SemaphoreType.DMA((HEADS,))],
        limit=60 << 20,
    )
    qkv = lax.all_to_all(qkv, "inner", 0, 0, tiled=True)
    far, q3_here, here = call(
        pick_chosen,
        [((2, half * 32, D), BF16), ((half * 32, D), BF16), ((half, HEADS, 2 * SLOTS, D), BF16)],
        (here,),
    )
    other_core = [(i, i ^ 1) for i in range(outer)]
    place = [(g, j) for g in range(groups) for j in range(NEAR)]
    far_a, far_b = [
        lax.ppermute(far, "outer", [(g * NEAR + j, (g + by[j // 2]) % groups * NEAR + j) for g, j in place])
        for by in ((4, 1, 2, 3), (0, 5, 6, 7))
    ]
    q3_there = lax.ppermute(q3_here, "outer", other_core)
    there = lax.ppermute(here, "outer", other_core)
    third = call(
        third_level,
        [((NEAR, HEADS, 8, D), F32)],
        (core, q3_here, q3_there, far_a, far_b),
        in_specs=[pl.BlockSpec(memory_space=pltpu.SMEM)] + vmem(4),
        out_specs=[anywhere],
        scratch=[pltpu.VMEM((NEAR, HEADS, 8, D), F32), pltpu.SemaphoreType.DMA((NEAR,))],
        flops=1 << 32,
    )
    third = lax.all_to_all(third, "outer", 0, 0, tiled=True, axis_index_groups=near_groups)
    o, lse = call(
        two_levels,
        [((HEADS, ROWS, D), BF16), ((HEADS, 8, D), F32)],
        (qkv, here, there),
        in_specs=vmem(2) + [anywhere],
        scratch=[pltpu.VMEM((HEADS * ROWS, 2 * D), BF16)] * 4
        + [pltpu.VMEM((2, ROWS, HEADS * ROWS), F32), pltpu.VMEM((2, ROWS, D), F32), pltpu.VMEM((3, ROWS, D), F32)]
        + [pltpu.VMEM((half, HEADS, 2 * SLOTS, D), BF16), pltpu.SemaphoreType.DMA],
        flops=1 << 33,
    )
    o = call(
        merge_third,
        [((HEADS, ROWS, D), BF16)],
        (lse, third, o),
        grid=(1,),
        in_specs=[whole(HEADS, 8, D), whole(NEAR, HEADS, 8, D), whole(HEADS, 16, D)],
        out_specs=[whole(HEADS, 16, D)],
        aliases={2: 0},
    )
    o = lax.all_to_all(o, "inner", 0, 0, tiled=True)
    return call(
        finish,
        [((ROWS, HEADS * D), BF16)],
        (o,),
        out_specs=[anywhere],
        scratch=[block, pltpu.SemaphoreType.DMA((4,))],
    )


def solution(mesh):
    rows = P(("outer", "inner"), None)
    return jax.shard_map(body, mesh=mesh, in_specs=(rows, rows, rows), out_specs=rows, check_vma=False)
```

```python
import functools
import math

import jax
import jax.numpy as jnp
from jax import lax
from jax.experimental import pallas as pl
from jax.experimental.pallas import tpu as pltpu
from jax.sharding import PartitionSpec as P

D = 128
HEADS = 8
ROWS = 256
SLOTS = 32
FAR = 4
NEAR = 8
GROUPS = 8
SCALE = D**-0.5 * math.log2(math.e)
LIMIT = 48 << 20

NT = (((1,), (1,)), ((), ()))
F32 = jnp.float32
BF16 = jnp.bfloat16


def place(t, head):
    u = t >> 3
    return (((t - head) & 7) << 5) + ((u & 7) << 2) + (u >> 3)


def to_order(head, places=ROWS):
    p = lax.broadcasted_iota(jnp.int32, (places, ROWS), 0)
    t = lax.broadcasted_iota(jnp.int32, (1, ROWS), 1)
    return jnp.where(p == place(t, head), 1.0, 0.0).astype(BF16)


def from_order(head):
    p = lax.broadcasted_iota(jnp.int32, (ROWS, ROWS), 1)
    t = lax.broadcasted_iota(jnp.int32, (ROWS, 1), 0)
    return jnp.where(p == place(t, head), 1.0, 0.0).astype(BF16)


def dot(a, b):
    return jnp.dot(a, b, preferred_element_type=F32)


def chosen_rows(q_hbm, k_hbm, v_hbm, near_hbm, q_scr, k_scr, v_scr, out_scr, in_sems, out_sems):
    copies = [pltpu.make_async_copy(k_hbm, k_scr, in_sems.at[0]), pltpu.make_async_copy(v_hbm, v_scr, in_sems.at[1])]
    copies += [
        pltpu.make_async_copy(q_hbm.at[pl.ds(64 * s, 16)], q_scr.at[pl.ds(16 * s, 16)], in_sems.at[2 + s])
        for s in range(FAR)
    ]
    for c in copies:
        c.start()
    written = []

    def send(i, at, rows):
        part = (slice(None), pl.ds(at, rows))
        for m in range(NEAR // 2):
            c = pltpu.make_async_copy(out_scr.at[part], near_hbm.at[(m, *part)], out_sems.at[i, m])
            c.start()
            written.append(c)

    for i, scr in enumerate((k_scr, v_scr)):
        copies[i].wait()
        for h in range(HEADS):
            got = dot(to_order(h, SLOTS), scr[:, h * D : (h + 1) * D])
            out_scr[h, i * SLOTS : (i + 1) * SLOTS] = got.astype(BF16)
        send(i, i * SLOTS, SLOTS)
    for c in copies[2:]:
        c.wait()
    slot = lax.broadcasted_iota(jnp.int32, (16, 16 * FAR), 0)
    row = lax.broadcasted_iota(jnp.int32, (16, 16 * FAR), 1)
    for h in range(HEADS):
        pick = jnp.where((row == 16 * slot + h) & (slot < FAR), 1.0, 0.0).astype(BF16)
        out_scr[h, 2 * SLOTS :] = dot(pick, q_scr[:, h * D : (h + 1) * D]).astype(BF16)
    send(2, 2 * SLOTS, 16)
    for c in written:
        c.wait()


def split_heads(q_hbm, k_hbm, v_hbm, qkv_hbm, q_scr, k_scr, v_scr, out_scr, in_sems, out_sems):
    pairs = ((k_hbm, k_scr), (v_hbm, v_scr), (q_hbm, q_scr))
    copies = [pltpu.make_async_copy(src, dst, in_sems.at[i]) for i, (src, dst) in enumerate(pairs)]
    for c in copies:
        c.start()
    for c in copies:
        c.wait()
    written = []
    for h in range(HEADS):
        cols = slice(h * D, (h + 1) * D)
        rows = jnp.concatenate([k_scr[:, cols], v_scr[:, cols], q_scr[:, cols]], axis=1)
        out = dot(to_order(h), rows).astype(BF16)
        for i in range(3):
            out_scr[h, i] = out[:, i * D : (i + 1) * D]
        c = pltpu.make_async_copy(out_scr.at[h], qkv_hbm.at[h], out_sems.at[h])
        c.start()
        written.append(c)
    for c in written:
        c.wait()


def pick_chosen(near_ref, far_ref, q3_ref, kv_ref):
    kv_ref[...] = near_ref[:, :, : 2 * SLOTS]
    a = lax.broadcasted_iota(jnp.int32, (HEADS * FAR, ROWS), 0)
    b = lax.broadcasted_iota(jnp.int32, (HEADS * FAR, ROWS), 1)
    pick = jnp.where(b == ((a >> 2) << 5) + (a & 3), 1.0, 0.0).astype(BF16)
    pick16 = jnp.where(b[:, : ROWS // 2] == ((a[:, : ROWS // 2] >> 2) << 4) + (a[:, : ROWS // 2] & 3), 1.0, 0.0)
    pick16 = pick16.astype(BF16)
    for m in range(NEAR // 2):
        k2 = near_ref[m, :, :SLOTS].reshape(ROWS, D)
        v2 = near_ref[m, :, SLOTS : 2 * SLOTS].reshape(ROWS, D)
        got = dot(pick, jnp.concatenate([k2, v2], axis=1)).astype(BF16)
        far_ref[0, m * 32 : (m + 1) * 32] = got[:, :D]
        far_ref[1, m * 32 : (m + 1) * 32] = got[:, D:]
        q = near_ref[m, :, 2 * SLOTS :].reshape(HEADS * 16, D)
        q3_ref[m * 32 : (m + 1) * 32] = dot(pick16, q).astype(BF16)


def two_parts(q):
    scaled = q.astype(F32) * SCALE
    high = scaled.astype(BF16)
    low = (scaled - high.astype(F32)).astype(BF16)
    return jnp.concatenate([high, low], axis=1)


def twice(k):
    return jnp.concatenate([k, k], axis=1)


def with_ones(v):
    return jnp.concatenate([v, jnp.ones_like(v)], axis=1)


def attend(q, keys, values):
    s = lax.dot_general(q, keys, NT, preferred_element_type=F32)
    top = jnp.max(s, axis=1, keepdims=True)
    w = jnp.exp2(s - top).astype(BF16)
    o = dot(w, values)
    return jnp.broadcast_to(top, (q.shape[0], D)), o[:, D:], o[:, :D]


def merge(top_a, total_a, part_a, top_b, total_b, part_b):
    peak = jnp.maximum(top_a, top_b)
    a, b = jnp.exp2(top_a - peak), jnp.exp2(top_b - peak)
    return peak, a * total_a + b * total_b, a * part_a + b * part_b


def two_levels(qkv_ref, here_ref, there_hbm, o_ref, lse_ref, k1, v1, k2, v2, s_scr, top_scr, first, there_ref, sem):
    fetch = pltpu.make_async_copy(there_hbm, there_ref, sem)
    fetch.start()
    half = NEAR // 2
    for s in range(HEADS):
        rows = slice(s * ROWS, (s + 1) * ROWS)
        k1[rows, :] = twice(qkv_ref[s, 0])
        v1[rows, :] = with_ones(qkv_ref[s, 1])

    def scores(tile):
        if tile < HEADS:
            q, keys = qkv_ref[tile, 2], k1
        else:
            q, keys = qkv_ref[:, 2, :SLOTS].reshape(ROWS, D), k2
        x = lax.dot_general(two_parts(q), keys[...], NT, preferred_element_type=F32)
        s_scr[tile % 2] = x
        top_scr[tile % 2] = jnp.broadcast_to(jnp.max(x, axis=1, keepdims=True), (ROWS, D))

    def weigh(tile):
        top = top_scr[tile % 2]
        w = jnp.exp2(s_scr[tile % 2] - top[:, :1]).astype(BF16)
        o = dot(w, (v1 if tile < HEADS else v2)[...])
        part, total = o[:, :D], o[:, D:]
        if tile < HEADS:
            o_ref[tile, SLOTS:] = (part[SLOTS:] / total[SLOTS:]).astype(BF16)
            rows = slice(tile * SLOTS, (tile + 1) * SLOTS)
            for i, x in enumerate((top, total, part)):
                first[i, rows] = x[:SLOTS]
        else:
            top, total, part = merge(first[0], first[1], first[2], top, total, part)
            o_ref[:, :SLOTS] = (part / total).astype(BF16).reshape(HEADS, SLOTS, D)
            lse_ref[...] = (top + jnp.log2(total)).reshape(HEADS, SLOTS, D)[:, :8]

    scores(0)
    fetch.wait()
    for i, ref in enumerate((here_ref, there_ref)):
        for m in range(half):
            at = (i * half + m) * ROWS
            k2[at : at + ROWS, :] = twice(ref[m, :, :SLOTS].reshape(ROWS, D))
            v2[at : at + ROWS, :] = with_ones(ref[m, :, SLOTS : 2 * SLOTS].reshape(ROWS, D))
    for tile in range(HEADS + 1):
        if tile < HEADS:
            scores(tile + 1)
        weigh(tile)


def merge_third(lse_ref, third_ref, o_in, o_ref):
    o = o_in[...].astype(F32)
    base = o[:, :8].reshape(HEADS * 8, D)
    parts = [third_ref[j].reshape(HEADS * 8, D) for j in range(NEAR)]
    sums = [lse_ref[...].reshape(HEADS * 8, D)] + [pltpu.roll(x, HEADS * 8 - 4, 0) for x in parts]
    peak = functools.reduce(jnp.maximum, sums)
    weights = [jnp.exp2(x - peak) for x in sums]
    last = sum(w * x for w, x in zip(weights, [base] + parts)) / sum(weights)
    row = lax.broadcasted_iota(jnp.int32, (HEADS * 8, D), 0) & 7
    last = jnp.where(row < FAR, last, base).reshape(HEADS, 8, D)
    o_ref[...] = jnp.concatenate([last, o[:, 8:]], axis=1).astype(BF16)


def third_level(core_ref, here_ref, there_ref, far_a, far_b, third_hbm, third_scr, sems):
    half = NEAR // 2
    n = half * HEADS * FAR
    a = lax.broadcasted_iota(jnp.int32, (2 * n, n), 0)
    b = lax.broadcasted_iota(jnp.int32, (2 * n, n), 1)
    pick = jnp.where(b == ((a >> 3) << 2) + (a & 3), 1.0, 0.0).astype(BF16)
    q3 = jnp.concatenate([dot(pick, here_ref[...]), dot(pick, there_ref[...])], axis=0).astype(BF16)
    k3 = jnp.concatenate([far_a[0], far_b[0]], axis=0)
    v3 = jnp.concatenate([far_a[1], far_b[1]], axis=0)
    level3 = attend(two_parts(q3), twice(k3), with_ones(v3))
    row = lax.broadcasted_iota(jnp.int32, (HEADS * 8, D), 0) & 7
    core = core_ref[0]
    written = []
    for j in range(NEAR):
        t, l, o = [x[j * 64 : (j + 1) * 64] for x in level3]
        at = 2 * j + core if j < half else 2 * (j - half) + 1 - core
        third_scr[j] = jnp.where(row < 4, o / l, t + jnp.log2(l)).reshape(HEADS, 8, D)
        c = pltpu.make_async_copy(third_scr.at[j], third_hbm.at[at], sems.at[j])
        c.start()
        written.append(c)
    for c in written:
        c.wait()


def finish(o_ref, out_hbm, out_scr, sems):
    orders = [from_order(h) for h in range(HEADS)]
    written = []
    for i in range(4):
        rows = slice(i * ROWS // 4, (i + 1) * ROWS // 4)
        for h in range(HEADS):
            out_scr[rows, h * D : (h + 1) * D] = dot(orders[h][rows], o_ref[h]).astype(BF16)
        c = pltpu.make_async_copy(out_scr.at[rows], out_hbm.at[rows], sems.at[i])
        c.start()
        written.append(c)
    for c in written:
        c.wait()


def vmem(n):
    return [pl.BlockSpec(memory_space=pltpu.VMEM)] * n


def call(kernel, outs, ins, scratch=(), in_specs=None, out_specs=None, aliases=None, flops=0, grid=None, limit=LIMIT):
    shapes = [jax.ShapeDtypeStruct(s, d) for s, d in outs]
    extra = {} if grid is None else {"grid": grid}
    got = pl.pallas_call(
        kernel,
        out_shape=shapes,
        in_specs=in_specs or vmem(len(ins)),
        out_specs=out_specs or vmem(len(outs)),
        scratch_shapes=list(scratch),
        input_output_aliases=aliases or {},
        compiler_params=pltpu.CompilerParams(vmem_limit_bytes=limit),
        cost_estimate=pl.CostEstimate(flops=flops, bytes_accessed=1 << 20, transcendentals=0),
        **extra,
    )(*ins)
    return got if len(outs) > 1 else got[0]


def whole(*shape):
    return pl.BlockSpec(shape, lambda i: (0,) * len(shape))


def body(queries, keys, values):
    outer = lax.axis_size("outer")
    groups = outer // NEAR
    half = NEAR // 2
    near_groups = [[g * NEAR + j for j in range(NEAR)] for g in range(groups)]
    same_core = [
        [(g * NEAR + 2 * m + c) * HEADS + i for m in range(half) for i in range(HEADS)]
        for g in range(groups)
        for c in range(2)
    ]
    core = (lax.axis_index("outer") % 2).astype(jnp.int32).reshape(1)
    anywhere = pl.BlockSpec(memory_space=pl.ANY)
    block = pltpu.VMEM((ROWS, HEADS * D), BF16)

    near = call(
        chosen_rows,
        [((half, HEADS, 80, D), BF16)],
        (queries, keys, values),
        in_specs=[anywhere] * 3,
        out_specs=[anywhere],
        scratch=[
            pltpu.VMEM((16 * FAR, HEADS * D), BF16),
            block,
            block,
            pltpu.VMEM((HEADS, 80, D), BF16),
            pltpu.SemaphoreType.DMA((2 + FAR,)),
            pltpu.SemaphoreType.DMA((3, half)),
        ],
        limit=60 << 20,
    )
    near = near.reshape(half * HEADS, 80, D)
    here = lax.all_to_all(near, ("outer", "inner"), 0, 0, tiled=True, axis_index_groups=same_core)
    here = here.reshape(half, HEADS, 80, D)
    qkv = call(
        split_heads,
        [((HEADS, 3, ROWS, D), BF16)],
        (queries, keys, values),
        in_specs=[anywhere] * 3,
        out_specs=[anywhere],
        scratch=[block] * 3
        + [pltpu.VMEM((HEADS, 3, ROWS, D), BF16), pltpu.SemaphoreType.DMA((3,)), pltpu.SemaphoreType.DMA((HEADS,))],
        limit=60 << 20,
    )
    qkv = lax.all_to_all(qkv, "inner", 0, 0, tiled=True)
    far, q3_here, here = call(
        pick_chosen,
        [((2, half * 32, D), BF16), ((half * 32, D), BF16), ((half, HEADS, 2 * SLOTS, D), BF16)],
        (here,),
    )
    other_core = [(i, i ^ 1) for i in range(outer)]
    place = [(g, j) for g in range(groups) for j in range(NEAR)]
    far_a, far_b = [
        lax.ppermute(far, "outer", [(g * NEAR + j, (g + by[j // 2]) % groups * NEAR + j) for g, j in place])
        for by in ((4, 1, 2, 3), (0, 5, 6, 7))
    ]
    q3_there = lax.ppermute(q3_here, "outer", other_core)
    there = lax.ppermute(here, "outer", other_core)
    third = call(
        third_level,
        [((NEAR, HEADS, 8, D), F32)],
        (core, q3_here, q3_there, far_a, far_b),
        in_specs=[pl.BlockSpec(memory_space=pltpu.SMEM)] + vmem(4),
        out_specs=[anywhere],
        scratch=[pltpu.VMEM((NEAR, HEADS, 8, D), F32), pltpu.SemaphoreType.DMA((NEAR,))],
        flops=1 << 32,
    )
    third = lax.all_to_all(third, "outer", 0, 0, tiled=True, axis_index_groups=near_groups)
    o, lse = call(
        two_levels,
        [((HEADS, ROWS, D), BF16), ((HEADS, 8, D), F32)],
        (qkv, here, there),
        in_specs=vmem(2) + [anywhere],
        scratch=[pltpu.VMEM((HEADS * ROWS, 2 * D), BF16)] * 4
        + [pltpu.VMEM((2, ROWS, HEADS * ROWS), F32), pltpu.VMEM((2, ROWS, D), F32), pltpu.VMEM((3, ROWS, D), F32)]
        + [pltpu.VMEM((half, HEADS, 2 * SLOTS, D), BF16), pltpu.SemaphoreType.DMA],
        flops=1 << 33,
    )
    o = call(
        merge_third,
        [((HEADS, ROWS, D), BF16)],
        (lse, third, o),
        grid=(1,),
        in_specs=[whole(HEADS, 8, D), whole(NEAR, HEADS, 8, D), whole(HEADS, 16, D)],
        out_specs=[whole(HEADS, 16, D)],
        aliases={2: 0},
    )
    o = lax.all_to_all(o, "inner", 0, 0, tiled=True)
    return call(
        finish,
        [((ROWS, HEADS * D), BF16)],
        (o,),
        out_specs=[anywhere],
        scratch=[block, pltpu.SemaphoreType.DMA((4,))],
    )


def solution(mesh):
    rows = P(("outer", "inner"), None)
    return jax.shard_map(body, mesh=mesh, in_specs=(rows, rows, rows), out_specs=rows, check_vma=False)
```

```python
import functools
import math

import jax
import jax.numpy as jnp
from jax import lax
from jax.experimental import pallas as pl
from jax.experimental.pallas import tpu as pltpu
from jax.sharding import PartitionSpec as P

D = 128
HEADS = 8
ROWS = 256
SLOTS = 32
FAR = 4
NEAR = 8
GROUPS = 8
SCALE = D**-0.5 * math.log2(math.e)
LIMIT = 48 << 20

NT = (((1,), (1,)), ((), ()))
F32 = jnp.float32
BF16 = jnp.bfloat16


def place(t, head):
    u = t >> 3
    return (((t - head) & 7) << 5) + ((u & 7) << 2) + (u >> 3)


def to_order(head, places=ROWS):
    p = lax.broadcasted_iota(jnp.int32, (places, ROWS), 0)
    t = lax.broadcasted_iota(jnp.int32, (1, ROWS), 1)
    return jnp.where(p == place(t, head), 1.0, 0.0).astype(BF16)


def from_order(head):
    p = lax.broadcasted_iota(jnp.int32, (ROWS, ROWS), 1)
    t = lax.broadcasted_iota(jnp.int32, (ROWS, 1), 0)
    return jnp.where(p == place(t, head), 1.0, 0.0).astype(BF16)


def dot(a, b):
    return jnp.dot(a, b, preferred_element_type=F32)


def chosen_rows(q_hbm, k_hbm, v_hbm, near_hbm, q_scr, k_scr, v_scr, out_scr, in_sems, out_sems):
    copies = [pltpu.make_async_copy(k_hbm, k_scr, in_sems.at[0]), pltpu.make_async_copy(v_hbm, v_scr, in_sems.at[1])]
    copies += [
        pltpu.make_async_copy(q_hbm.at[pl.ds(64 * s, 16)], q_scr.at[pl.ds(16 * s, 16)], in_sems.at[2 + s])
        for s in range(FAR)
    ]
    for c in copies:
        c.start()
    written = []

    def send(i, at, rows):
        part = (slice(None), pl.ds(at, rows))
        for m in range(NEAR // 2):
            c = pltpu.make_async_copy(out_scr.at[part], near_hbm.at[(m, *part)], out_sems.at[i, m])
            c.start()
            written.append(c)

    for i, scr in enumerate((k_scr, v_scr)):
        copies[i].wait()
        for h in range(HEADS):
            got = dot(to_order(h, SLOTS), scr[:, h * D : (h + 1) * D])
            out_scr[h, i * SLOTS : (i + 1) * SLOTS] = got.astype(BF16)
        send(i, i * SLOTS, SLOTS)
    for c in copies[2:]:
        c.wait()
    slot = lax.broadcasted_iota(jnp.int32, (16, 16 * FAR), 0)
    row = lax.broadcasted_iota(jnp.int32, (16, 16 * FAR), 1)
    for h in range(HEADS):
        pick = jnp.where((row == 16 * slot + h) & (slot < FAR), 1.0, 0.0).astype(BF16)
        out_scr[h, 2 * SLOTS :] = dot(pick, q_scr[:, h * D : (h + 1) * D]).astype(BF16)
    send(2, 2 * SLOTS, 16)
    for c in written:
        c.wait()


def split_heads(q_hbm, k_hbm, v_hbm, qkv_hbm, q_scr, k_scr, v_scr, out_scr, in_sems, out_sems):
    pairs = ((k_hbm, k_scr), (v_hbm, v_scr), (q_hbm, q_scr))
    copies = [pltpu.make_async_copy(src, dst, in_sems.at[i]) for i, (src, dst) in enumerate(pairs)]
    for c in copies:
        c.start()
    for c in copies:
        c.wait()
    written = []
    for h in range(HEADS):
        cols = slice(h * D, (h + 1) * D)
        rows = jnp.concatenate([k_scr[:, cols], v_scr[:, cols], q_scr[:, cols]], axis=1)
        out = dot(to_order(h), rows).astype(BF16)
        for i in range(3):
            out_scr[h, i] = out[:, i * D : (i + 1) * D]
        c = pltpu.make_async_copy(out_scr.at[h], qkv_hbm.at[h], out_sems.at[h])
        c.start()
        written.append(c)
    for c in written:
        c.wait()


def pick_chosen(near_ref, far_ref, q3_ref, kv_ref):
    kv_ref[...] = near_ref[:, :, : 2 * SLOTS]
    a = lax.broadcasted_iota(jnp.int32, (HEADS * FAR, ROWS), 0)
    b = lax.broadcasted_iota(jnp.int32, (HEADS * FAR, ROWS), 1)
    pick = jnp.where(b == ((a >> 2) << 5) + (a & 3), 1.0, 0.0).astype(BF16)
    pick16 = jnp.where(b[:, : ROWS // 2] == ((a[:, : ROWS // 2] >> 2) << 4) + (a[:, : ROWS // 2] & 3), 1.0, 0.0)
    pick16 = pick16.astype(BF16)
    for m in range(NEAR // 2):
        k2 = near_ref[m, :, :SLOTS].reshape(ROWS, D)
        v2 = near_ref[m, :, SLOTS : 2 * SLOTS].reshape(ROWS, D)
        got = dot(pick, jnp.concatenate([k2, v2], axis=1)).astype(BF16)
        far_ref[0, m * 32 : (m + 1) * 32] = got[:, :D]
        far_ref[1, m * 32 : (m + 1) * 32] = got[:, D:]
        q = near_ref[m, :, 2 * SLOTS :].reshape(HEADS * 16, D)
        q3_ref[m * 32 : (m + 1) * 32] = dot(pick16, q).astype(BF16)


def two_parts(q):
    scaled = q.astype(F32) * SCALE
    high = scaled.astype(BF16)
    low = (scaled - high.astype(F32)).astype(BF16)
    return jnp.concatenate([high, low], axis=1)


def twice(k):
    return jnp.concatenate([k, k], axis=1)


def with_ones(v):
    return jnp.concatenate([v, jnp.ones_like(v)], axis=1)


def attend(q, keys, values):
    s = lax.dot_general(q, keys, NT, preferred_element_type=F32)
    top = jnp.max(s, axis=1, keepdims=True)
    w = jnp.exp2(s - top).astype(BF16)
    o = dot(w, values)
    return jnp.broadcast_to(top, (q.shape[0], D)), o[:, D:], o[:, :D]


def merge(top_a, total_a, part_a, top_b, total_b, part_b):
    peak = jnp.maximum(top_a, top_b)
    a, b = jnp.exp2(top_a - peak), jnp.exp2(top_b - peak)
    return peak, a * total_a + b * total_b, a * part_a + b * part_b


def two_levels(qkv_ref, here_ref, there_hbm, o_ref, lse_ref, k1, v1, k2, v2, s_scr, top_scr, first, there_ref, sem):
    fetch = pltpu.make_async_copy(there_hbm, there_ref, sem)
    fetch.start()
    half = NEAR // 2
    for s in range(HEADS):
        rows = slice(s * ROWS, (s + 1) * ROWS)
        k1[rows, :] = twice(qkv_ref[s, 0])
        v1[rows, :] = with_ones(qkv_ref[s, 1])

    def scores(tile):
        if tile < HEADS:
            q, keys = qkv_ref[tile, 2], k1
        else:
            q, keys = qkv_ref[:, 2, :SLOTS].reshape(ROWS, D), k2
        x = lax.dot_general(two_parts(q), keys[...], NT, preferred_element_type=F32)
        s_scr[tile % 2] = x
        top_scr[tile % 2] = jnp.broadcast_to(jnp.max(x, axis=1, keepdims=True), (ROWS, D))

    def weigh(tile):
        top = top_scr[tile % 2]
        w = jnp.exp2(s_scr[tile % 2] - top[:, :1]).astype(BF16)
        o = dot(w, (v1 if tile < HEADS else v2)[...])
        part, total = o[:, :D], o[:, D:]
        if tile < HEADS:
            o_ref[tile, SLOTS:] = (part[SLOTS:] / total[SLOTS:]).astype(BF16)
            rows = slice(tile * SLOTS, (tile + 1) * SLOTS)
            for i, x in enumerate((top, total, part)):
                first[i, rows] = x[:SLOTS]
        else:
            top, total, part = merge(first[0], first[1], first[2], top, total, part)
            o_ref[:, :SLOTS] = (part / total).astype(BF16).reshape(HEADS, SLOTS, D)
            lse_ref[...] = (top + jnp.log2(total)).reshape(HEADS, SLOTS, D)[:, :8]

    scores(0)
    fetch.wait()
    for i, ref in enumerate((here_ref, there_ref)):
        for m in range(half):
            at = (i * half + m) * ROWS
            k2[at : at + ROWS, :] = twice(ref[m, :, :SLOTS].reshape(ROWS, D))
            v2[at : at + ROWS, :] = with_ones(ref[m, :, SLOTS : 2 * SLOTS].reshape(ROWS, D))
    for tile in range(HEADS + 1):
        if tile < HEADS:
            scores(tile + 1)
        weigh(tile)


def merge_third(lse_ref, third_ref, o_in, o_ref):
    o = o_in[...].astype(F32)
    base = o[:, :8].reshape(HEADS * 8, D)
    parts = [third_ref[j].reshape(HEADS * 8, D) for j in range(NEAR)]
    sums = [lse_ref[...].reshape(HEADS * 8, D)] + [pltpu.roll(x, HEADS * 8 - 4, 0) for x in parts]
    peak = functools.reduce(jnp.maximum, sums)
    weights = [jnp.exp2(x - peak) for x in sums]
    last = sum(w * x for w, x in zip(weights, [base] + parts)) / sum(weights)
    row = lax.broadcasted_iota(jnp.int32, (HEADS * 8, D), 0) & 7
    last = jnp.where(row < FAR, last, base).reshape(HEADS, 8, D)
    o_ref[...] = jnp.concatenate([last, o[:, 8:]], axis=1).astype(BF16)


def third_level(core_ref, here_ref, there_ref, far_a, far_b, third_hbm, third_scr, sems):
    half = NEAR // 2
    n = half * HEADS * FAR
    a = lax.broadcasted_iota(jnp.int32, (2 * n, n), 0)
    b = lax.broadcasted_iota(jnp.int32, (2 * n, n), 1)
    pick = jnp.where(b == ((a >> 3) << 2) + (a & 3), 1.0, 0.0).astype(BF16)
    q3 = jnp.concatenate([dot(pick, here_ref[...]), dot(pick, there_ref[...])], axis=0).astype(BF16)
    k3 = jnp.concatenate([far_a[0], far_b[0]], axis=0)
    v3 = jnp.concatenate([far_a[1], far_b[1]], axis=0)
    level3 = attend(two_parts(q3), twice(k3), with_ones(v3))
    row = lax.broadcasted_iota(jnp.int32, (HEADS * 8, D), 0) & 7
    core = core_ref[0]
    written = []
    for j in range(NEAR):
        t, l, o = [x[j * 64 : (j + 1) * 64] for x in level3]
        at = 2 * j + core if j < half else 2 * (j - half) + 1 - core
        third_scr[j] = jnp.where(row < 4, o / l, t + jnp.log2(l)).reshape(HEADS, 8, D)
        c = pltpu.make_async_copy(third_scr.at[j], third_hbm.at[at], sems.at[j])
        c.start()
        written.append(c)
    for c in written:
        c.wait()


def finish(o_ref, out_hbm, out_scr, sems):
    orders = [from_order(h) for h in range(HEADS)]
    written = []
    for i in range(4):
        rows = slice(i * ROWS // 4, (i + 1) * ROWS // 4)
        for h in range(HEADS):
            out_scr[rows, h * D : (h + 1) * D] = dot(orders[h][rows], o_ref[h]).astype(BF16)
        c = pltpu.make_async_copy(out_scr.at[rows], out_hbm.at[rows], sems.at[i])
        c.start()
        written.append(c)
    for c in written:
        c.wait()


def vmem(n):
    return [pl.BlockSpec(memory_space=pltpu.VMEM)] * n


def call(kernel, outs, ins, scratch=(), in_specs=None, out_specs=None, aliases=None, flops=0, grid=None, limit=LIMIT):
    shapes = [jax.ShapeDtypeStruct(s, d) for s, d in outs]
    extra = {} if grid is None else {"grid": grid}
    got = pl.pallas_call(
        kernel,
        out_shape=shapes,
        in_specs=in_specs or vmem(len(ins)),
        out_specs=out_specs or vmem(len(outs)),
        scratch_shapes=list(scratch),
        input_output_aliases=aliases or {},
        compiler_params=pltpu.CompilerParams(vmem_limit_bytes=limit),
        cost_estimate=pl.CostEstimate(flops=flops, bytes_accessed=1 << 20, transcendentals=0),
        **extra,
    )(*ins)
    return got if len(outs) > 1 else got[0]


def whole(*shape):
    return pl.BlockSpec(shape, lambda i: (0,) * len(shape))


def body(queries, keys, values):
    outer = lax.axis_size("outer")
    groups = outer // NEAR
    half = NEAR // 2
    near_groups = [[g * NEAR + j for j in range(NEAR)] for g in range(groups)]
    same_core = [
        [(g * NEAR + 2 * m + c) * HEADS + i for m in range(half) for i in range(HEADS)]
        for g in range(groups)
        for c in range(2)
    ]
    core = (lax.axis_index("outer") % 2).astype(jnp.int32).reshape(1)
    anywhere = pl.BlockSpec(memory_space=pl.ANY)
    block = pltpu.VMEM((ROWS, HEADS * D), BF16)

    near = call(
        chosen_rows,
        [((half, HEADS, 80, D), BF16)],
        (queries, keys, values),
        in_specs=[anywhere] * 3,
        out_specs=[anywhere],
        scratch=[
            pltpu.VMEM((16 * FAR, HEADS * D), BF16),
            block,
            block,
            pltpu.VMEM((HEADS, 80, D), BF16),
            pltpu.SemaphoreType.DMA((2 + FAR,)),
            pltpu.SemaphoreType.DMA((3, half)),
        ],
        limit=60 << 20,
    )
    near = near.reshape(half * HEADS, 80, D)
    here = lax.all_to_all(near, ("outer", "inner"), 0, 0, tiled=True, axis_index_groups=same_core)
    here = here.reshape(half, HEADS, 80, D)
    qkv = call(
        split_heads,
        [((HEADS, 3, ROWS, D), BF16)],
        (queries, keys, values),
        in_specs=[anywhere] * 3,
        out_specs=[anywhere],
        scratch=[block] * 3
        + [pltpu.VMEM((HEADS, 3, ROWS, D), BF16), pltpu.SemaphoreType.DMA((3,)), pltpu.SemaphoreType.DMA((HEADS,))],
        limit=60 << 20,
    )
    qkv = lax.all_to_all(qkv, "inner", 0, 0, tiled=True)
    far, q3_here, here = call(
        pick_chosen,
        [((2, half * 32, D), BF16), ((half * 32, D), BF16), ((half, HEADS, 2 * SLOTS, D), BF16)],
        (here,),
    )
    other_core = [(i, i ^ 1) for i in range(outer)]
    place = [(g, j) for g in range(groups) for j in range(NEAR)]
    far_a, far_b = [
        lax.ppermute(far, "outer", [(g * NEAR + j, (g + by[j // 2]) % groups * NEAR + j) for g, j in place])
        for by in ((4, 3, 5, 2), (0, 7, 1, 6))
    ]
    q3_there = lax.ppermute(q3_here, "outer", other_core)
    there = lax.ppermute(here, "outer", other_core)
    third = call(
        third_level,
        [((NEAR, HEADS, 8, D), F32)],
        (core, q3_here, q3_there, far_a, far_b),
        in_specs=[pl.BlockSpec(memory_space=pltpu.SMEM)] + vmem(4),
        out_specs=[anywhere],
        scratch=[pltpu.VMEM((NEAR, HEADS, 8, D), F32), pltpu.SemaphoreType.DMA((NEAR,))],
        flops=1 << 32,
    )
    third = lax.all_to_all(third, "outer", 0, 0, tiled=True, axis_index_groups=near_groups)
    o, lse = call(
        two_levels,
        [((HEADS, ROWS, D), BF16), ((HEADS, 8, D), F32)],
        (qkv, here, there),
        in_specs=vmem(2) + [anywhere],
        scratch=[pltpu.VMEM((HEADS * ROWS, 2 * D), BF16)] * 4
        + [pltpu.VMEM((2, ROWS, HEADS * ROWS), F32), pltpu.VMEM((2, ROWS, D), F32), pltpu.VMEM((3, ROWS, D), F32)]
        + [pltpu.VMEM((half, HEADS, 2 * SLOTS, D), BF16), pltpu.SemaphoreType.DMA],
        flops=1 << 33,
    )
    o = call(
        merge_third,
        [((HEADS, ROWS, D), BF16)],
        (lse, third, o),
        grid=(1,),
        in_specs=[whole(HEADS, 8, D), whole(NEAR, HEADS, 8, D), whole(HEADS, 16, D)],
        out_specs=[whole(HEADS, 16, D)],
        aliases={2: 0},
    )
    o = lax.all_to_all(o, "inner", 0, 0, tiled=True)
    return call(
        finish,
        [((ROWS, HEADS * D), BF16)],
        (o,),
        out_specs=[anywhere],
        scratch=[block, pltpu.SemaphoreType.DMA((4,))],
    )


def solution(mesh):
    rows = P(("outer", "inner"), None)
    return jax.shard_map(body, mesh=mesh, in_specs=(rows, rows, rows), out_specs=rows, check_vma=False)
```

```python
import functools
import math

import jax
import jax.numpy as jnp
from jax import lax
from jax.experimental import pallas as pl
from jax.experimental.pallas import tpu as pltpu
from jax.sharding import PartitionSpec as P

D = 128
HEADS = 8
ROWS = 256
SLOTS = 32
FAR = 4
NEAR = 8
GROUPS = 8
SCALE = D**-0.5 * math.log2(math.e)
LIMIT = 48 << 20

NT = (((1,), (1,)), ((), ()))
F32 = jnp.float32
BF16 = jnp.bfloat16


def place(t, head):
    u = t >> 3
    return (((t - head) & 7) << 5) + ((u & 7) << 2) + (u >> 3)


def to_order(head, places=ROWS):
    p = lax.broadcasted_iota(jnp.int32, (places, ROWS), 0)
    t = lax.broadcasted_iota(jnp.int32, (1, ROWS), 1)
    return jnp.where(p == place(t, head), 1.0, 0.0).astype(BF16)


def from_order(head):
    p = lax.broadcasted_iota(jnp.int32, (ROWS, ROWS), 1)
    t = lax.broadcasted_iota(jnp.int32, (ROWS, 1), 0)
    return jnp.where(p == place(t, head), 1.0, 0.0).astype(BF16)


def dot(a, b):
    return jnp.dot(a, b, preferred_element_type=F32)


def chosen_rows(q_hbm, k_hbm, v_hbm, near_hbm, q_scr, k_scr, v_scr, out_scr, in_sems, out_sems):
    copies = [pltpu.make_async_copy(k_hbm, k_scr, in_sems.at[0]), pltpu.make_async_copy(v_hbm, v_scr, in_sems.at[1])]
    copies += [
        pltpu.make_async_copy(q_hbm.at[pl.ds(64 * s, 16)], q_scr.at[pl.ds(16 * s, 16)], in_sems.at[2 + s])
        for s in range(FAR)
    ]
    for c in copies:
        c.start()
    written = []

    def send(i, at, rows):
        part = (slice(None), pl.ds(at, rows))
        for m in range(NEAR // 2):
            c = pltpu.make_async_copy(out_scr.at[part], near_hbm.at[(m, *part)], out_sems.at[i, m])
            c.start()
            written.append(c)

    for i, scr in enumerate((k_scr, v_scr)):
        copies[i].wait()
        for h in range(HEADS):
            got = dot(to_order(h, SLOTS), scr[:, h * D : (h + 1) * D])
            out_scr[h, i * SLOTS : (i + 1) * SLOTS] = got.astype(BF16)
        send(i, i * SLOTS, SLOTS)
    for c in copies[2:]:
        c.wait()
    slot = lax.broadcasted_iota(jnp.int32, (16, 16 * FAR), 0)
    row = lax.broadcasted_iota(jnp.int32, (16, 16 * FAR), 1)
    for h in range(HEADS):
        pick = jnp.where((row == 16 * slot + h) & (slot < FAR), 1.0, 0.0).astype(BF16)
        out_scr[h, 2 * SLOTS :] = dot(pick, q_scr[:, h * D : (h + 1) * D]).astype(BF16)
    send(2, 2 * SLOTS, 16)
    for c in written:
        c.wait()


def split_heads(q_hbm, k_hbm, v_hbm, qkv_hbm, q_scr, k_scr, v_scr, out_scr, in_sems, out_sems):
    pairs = ((k_hbm, k_scr), (v_hbm, v_scr), (q_hbm, q_scr))
    copies = [pltpu.make_async_copy(src, dst, in_sems.at[i]) for i, (src, dst) in enumerate(pairs)]
    for c in copies:
        c.start()
    for c in copies:
        c.wait()
    written = []
    for h in range(HEADS):
        cols = slice(h * D, (h + 1) * D)
        rows = jnp.concatenate([k_scr[:, cols], v_scr[:, cols], q_scr[:, cols]], axis=1)
        out = dot(to_order(h), rows).astype(BF16)
        for i in range(3):
            out_scr[h, i] = out[:, i * D : (i + 1) * D]
        c = pltpu.make_async_copy(out_scr.at[h], qkv_hbm.at[h], out_sems.at[h])
        c.start()
        written.append(c)
    for c in written:
        c.wait()


def pick_chosen(near_ref, far_ref, q3_ref, kv_ref):
    kv_ref[...] = near_ref[:, :, : 2 * SLOTS]
    a = lax.broadcasted_iota(jnp.int32, (HEADS * FAR, ROWS), 0)
    b = lax.broadcasted_iota(jnp.int32, (HEADS * FAR, ROWS), 1)
    pick = jnp.where(b == ((a >> 2) << 5) + (a & 3), 1.0, 0.0).astype(BF16)
    pick16 = jnp.where(b[:, : ROWS // 2] == ((a[:, : ROWS // 2] >> 2) << 4) + (a[:, : ROWS // 2] & 3), 1.0, 0.0)
    pick16 = pick16.astype(BF16)
    for m in range(NEAR // 2):
        k2 = near_ref[m, :, :SLOTS].reshape(ROWS, D)
        v2 = near_ref[m, :, SLOTS : 2 * SLOTS].reshape(ROWS, D)
        got = dot(pick, jnp.concatenate([k2, v2], axis=1)).astype(BF16)
        far_ref[0, m * 32 : (m + 1) * 32] = got[:, :D]
        far_ref[1, m * 32 : (m + 1) * 32] = got[:, D:]
        q = near_ref[m, :, 2 * SLOTS :].reshape(HEADS * 16, D)
        q3_ref[m * 32 : (m + 1) * 32] = dot(pick16, q).astype(BF16)


def two_parts(q):
    scaled = q.astype(F32) * SCALE
    high = scaled.astype(BF16)
    low = (scaled - high.astype(F32)).astype(BF16)
    return jnp.concatenate([high, low], axis=1)


def twice(k):
    return jnp.concatenate([k, k], axis=1)


def with_ones(v):
    return jnp.concatenate([v, jnp.ones_like(v)], axis=1)


def attend(q, keys, values):
    s = lax.dot_general(q, keys, NT, preferred_element_type=F32)
    top = jnp.max(s, axis=1, keepdims=True)
    w = jnp.exp2(s - top).astype(BF16)
    o = dot(w, values)
    return jnp.broadcast_to(top, (q.shape[0], D)), o[:, D:], o[:, :D]


def merge(top_a, total_a, part_a, top_b, total_b, part_b):
    peak = jnp.maximum(top_a, top_b)
    a, b = jnp.exp2(top_a - peak), jnp.exp2(top_b - peak)
    return peak, a * total_a + b * total_b, a * part_a + b * part_b


def two_levels(qkv_ref, here_ref, there_hbm, o_ref, lse_ref, k1, v1, k2, v2, s_scr, top_scr, first, there_ref, sem):
    fetch = pltpu.make_async_copy(there_hbm, there_ref, sem)
    fetch.start()
    half = NEAR // 2
    for s in range(HEADS):
        rows = slice(s * ROWS, (s + 1) * ROWS)
        k1[rows, :] = twice(qkv_ref[s, 0])
        v1[rows, :] = with_ones(qkv_ref[s, 1])

    def scores(tile):
        if tile < HEADS:
            q, keys = qkv_ref[tile, 2], k1
        else:
            q, keys = qkv_ref[:, 2, :SLOTS].reshape(ROWS, D), k2
        x = lax.dot_general(two_parts(q), keys[...], NT, preferred_element_type=F32)
        s_scr[tile % 2] = x
        top_scr[tile % 2] = jnp.broadcast_to(jnp.max(x, axis=1, keepdims=True), (ROWS, D))

    def weigh(tile):
        top = top_scr[tile % 2]
        w = jnp.exp2(s_scr[tile % 2] - top[:, :1]).astype(BF16)
        o = dot(w, (v1 if tile < HEADS else v2)[...])
        part, total = o[:, :D], o[:, D:]
        if tile < HEADS:
            o_ref[tile, SLOTS:] = (part[SLOTS:] / total[SLOTS:]).astype(BF16)
            rows = slice(tile * SLOTS, (tile + 1) * SLOTS)
            for i, x in enumerate((top, total, part)):
                first[i, rows] = x[:SLOTS]
        else:
            top, total, part = merge(first[0], first[1], first[2], top, total, part)
            o_ref[:, :SLOTS] = (part / total).astype(BF16).reshape(HEADS, SLOTS, D)
            lse_ref[...] = (top + jnp.log2(total)).reshape(HEADS, SLOTS, D)[:, :8]

    scores(0)
    fetch.wait()
    for i, ref in enumerate((here_ref, there_ref)):
        for m in range(half):
            at = (i * half + m) * ROWS
            k2[at : at + ROWS, :] = twice(ref[m, :, :SLOTS].reshape(ROWS, D))
            v2[at : at + ROWS, :] = with_ones(ref[m, :, SLOTS : 2 * SLOTS].reshape(ROWS, D))
    for tile in range(HEADS + 1):
        if tile < HEADS:
            scores(tile + 1)
        weigh(tile)


def merge_third(lse_ref, third_ref, o_in, o_ref):
    o = o_in[...].astype(F32)
    base = o[:, :8].reshape(HEADS * 8, D)
    parts = [third_ref[j].reshape(HEADS * 8, D) for j in range(NEAR)]
    sums = [lse_ref[...].reshape(HEADS * 8, D)] + [pltpu.roll(x, HEADS * 8 - 4, 0) for x in parts]
    peak = functools.reduce(jnp.maximum, sums)
    weights = [jnp.exp2(x - peak) for x in sums]
    last = sum(w * x for w, x in zip(weights, [base] + parts)) / sum(weights)
    row = lax.broadcasted_iota(jnp.int32, (HEADS * 8, D), 0) & 7
    last = jnp.where(row < FAR, last, base).reshape(HEADS, 8, D)
    o_ref[...] = jnp.concatenate([last, o[:, 8:]], axis=1).astype(BF16)


def third_level(core_ref, here_ref, there_ref, far_a, far_b, third_hbm, third_scr, sems):
    half = NEAR // 2
    n = half * HEADS * FAR
    a = lax.broadcasted_iota(jnp.int32, (2 * n, n), 0)
    b = lax.broadcasted_iota(jnp.int32, (2 * n, n), 1)
    pick = jnp.where(b == ((a >> 3) << 2) + (a & 3), 1.0, 0.0).astype(BF16)
    q3 = jnp.concatenate([dot(pick, here_ref[...]), dot(pick, there_ref[...])], axis=0).astype(BF16)
    k3 = jnp.concatenate([far_a[0], far_b[0]], axis=0)
    v3 = jnp.concatenate([far_a[1], far_b[1]], axis=0)
    level3 = attend(two_parts(q3), twice(k3), with_ones(v3))
    row = lax.broadcasted_iota(jnp.int32, (HEADS * 8, D), 0) & 7
    core = core_ref[0]
    written = []
    for j in range(NEAR):
        t, l, o = [x[j * 64 : (j + 1) * 64] for x in level3]
        at = 2 * j + core if j < half else 2 * (j - half) + 1 - core
        third_scr[j] = jnp.where(row < 4, o / l, t + jnp.log2(l)).reshape(HEADS, 8, D)
        c = pltpu.make_async_copy(third_scr.at[j], third_hbm.at[at], sems.at[j])
        c.start()
        written.append(c)
    for c in written:
        c.wait()


def finish(o_ref, out_hbm, out_scr, sems):
    orders = [from_order(h) for h in range(HEADS)]
    written = []
    for i in range(4):
        rows = slice(i * ROWS // 4, (i + 1) * ROWS // 4)
        for h in range(HEADS):
            out_scr[rows, h * D : (h + 1) * D] = dot(orders[h][rows], o_ref[h]).astype(BF16)
        c = pltpu.make_async_copy(out_scr.at[rows], out_hbm.at[rows], sems.at[i])
        c.start()
        written.append(c)
    for c in written:
        c.wait()


def vmem(n):
    return [pl.BlockSpec(memory_space=pltpu.VMEM)] * n


def call(kernel, outs, ins, scratch=(), in_specs=None, out_specs=None, aliases=None, flops=0, grid=None, limit=LIMIT):
    shapes = [jax.ShapeDtypeStruct(s, d) for s, d in outs]
    extra = {} if grid is None else {"grid": grid}
    got = pl.pallas_call(
        kernel,
        out_shape=shapes,
        in_specs=in_specs or vmem(len(ins)),
        out_specs=out_specs or vmem(len(outs)),
        scratch_shapes=list(scratch),
        input_output_aliases=aliases or {},
        compiler_params=pltpu.CompilerParams(vmem_limit_bytes=limit),
        cost_estimate=pl.CostEstimate(flops=flops, bytes_accessed=1 << 20, transcendentals=0),
        **extra,
    )(*ins)
    return got if len(outs) > 1 else got[0]


def whole(*shape):
    return pl.BlockSpec(shape, lambda i: (0,) * len(shape))


def body(queries, keys, values):
    outer = lax.axis_size("outer")
    groups = outer // NEAR
    half = NEAR // 2
    near_groups = [[g * NEAR + j for j in range(NEAR)] for g in range(groups)]
    same_core = [
        [(g * NEAR + 2 * m + c) * HEADS + i for m in range(half) for i in range(HEADS)]
        for g in range(groups)
        for c in range(2)
    ]
    core = (lax.axis_index("outer") % 2).astype(jnp.int32).reshape(1)
    anywhere = pl.BlockSpec(memory_space=pl.ANY)
    block = pltpu.VMEM((ROWS, HEADS * D), BF16)

    near = call(
        chosen_rows,
        [((half, HEADS, 80, D), BF16)],
        (queries, keys, values),
        in_specs=[anywhere] * 3,
        out_specs=[anywhere],
        scratch=[
            pltpu.VMEM((16 * FAR, HEADS * D), BF16),
            block,
            block,
            pltpu.VMEM((HEADS, 80, D), BF16),
            pltpu.SemaphoreType.DMA((2 + FAR,)),
            pltpu.SemaphoreType.DMA((3, half)),
        ],
        limit=60 << 20,
    )
    near = near.reshape(half * HEADS, 80, D)
    here = lax.all_to_all(near, ("outer", "inner"), 0, 0, tiled=True, axis_index_groups=same_core)
    here = here.reshape(half, HEADS, 80, D)
    qkv = call(
        split_heads,
        [((HEADS, 3, ROWS, D), BF16)],
        (queries, keys, values),
        in_specs=[anywhere] * 3,
        out_specs=[anywhere],
        scratch=[block] * 3
        + [pltpu.VMEM((HEADS, 3, ROWS, D), BF16), pltpu.SemaphoreType.DMA((3,)), pltpu.SemaphoreType.DMA((HEADS,))],
        limit=60 << 20,
    )
    qkv = lax.all_to_all(qkv, "inner", 0, 0, tiled=True)
    far, q3_here, here = call(
        pick_chosen,
        [((2, half * 32, D), BF16), ((half * 32, D), BF16), ((half, HEADS, 2 * SLOTS, D), BF16)],
        (here,),
    )
    other_core = [(i, i ^ 1) for i in range(outer)]
    place = [(g, j) for g in range(groups) for j in range(NEAR)]
    far_a, far_b = [
        lax.ppermute(far, "outer", [(g * NEAR + j, (g + by[j // 2]) % groups * NEAR + j) for g, j in place])
        for by in ((0, 1, 2, 3), (4, 5, 6, 7))
    ]
    q3_there = lax.ppermute(q3_here, "outer", other_core)
    there = lax.ppermute(here, "outer", other_core)
    third = call(
        third_level,
        [((NEAR, HEADS, 8, D), F32)],
        (core, q3_here, q3_there, far_a, far_b),
        in_specs=[pl.BlockSpec(memory_space=pltpu.SMEM)] + vmem(4),
        out_specs=[anywhere],
        scratch=[pltpu.VMEM((NEAR, HEADS, 8, D), F32), pltpu.SemaphoreType.DMA((NEAR,))],
        flops=1 << 32,
    )
    third = lax.all_to_all(third, "outer", 0, 0, tiled=True, axis_index_groups=near_groups)
    o, lse = call(
        two_levels,
        [((HEADS, ROWS, D), BF16), ((HEADS, 8, D), F32)],
        (qkv, here, there),
        in_specs=vmem(2) + [anywhere],
        scratch=[pltpu.VMEM((HEADS * ROWS, 2 * D), BF16)] * 4
        + [pltpu.VMEM((2, ROWS, HEADS * ROWS), F32), pltpu.VMEM((2, ROWS, D), F32), pltpu.VMEM((3, ROWS, D), F32)]
        + [pltpu.VMEM((half, HEADS, 2 * SLOTS, D), BF16), pltpu.SemaphoreType.DMA],
        flops=1 << 33,
    )
    o = call(
        merge_third,
        [((HEADS, ROWS, D), BF16)],
        (lse, third, o),
        grid=(1,),
        in_specs=[whole(HEADS, 8, D), whole(NEAR, HEADS, 8, D), whole(HEADS, 16, D)],
        out_specs=[whole(HEADS, 16, D)],
        aliases={2: 0},
    )
    o = lax.all_to_all(o, "inner", 0, 0, tiled=True)
    return call(
        finish,
        [((ROWS, HEADS * D), BF16)],
        (o,),
        out_specs=[anywhere],
        scratch=[block, pltpu.SemaphoreType.DMA((4,))],
    )


def solution(mesh):
    rows = P(("outer", "inner"), None)
    return jax.shard_map(body, mesh=mesh, in_specs=(rows, rows, rows), out_specs=rows, check_vma=False)
```
